32 devices in a mesh: section: 4 (over y, x), expert: 8 (over z, core).
Axes of the slice: x: 2, y: 2, z: 4, core: 2. Of those that a mesh axis runs over, the one named last changes fastest.
Arguments:
- hidden: bfloat16 [4, 512, 4096], P('section', 'expert'), may hold values from -6 to 6
- queries: bfloat16 [4, 512, 4096], P('section', 'expert'), may hold values from -10 to 10
- fresh_kv: bfloat16 [4, 2, 512, 256], P('section', None, 'expert'), may hold values from -10 to 10
- cache_kv: bfloat16 [4, 2, 256, 256], P('section', None, 'expert'), may hold values from -10 to 10
- cache_fill: int32 [4], P('section'), may hold values from 128 to 256, as said below
- out_proj: bfloat16 [4, 4096, 4096], P('section', 'expert'), may hold values from -0.375 to 0.375
- norm_gain: bfloat16 [4, 4096], P('section'), may hold values from 0.5 to 1.5
- router_weight: bfloat16 [4, 4096, 128], P('section'), may hold values from -3 to 3
- expert_labels: int32 [4, 512, 8], P('section', 'expert'), may hold values from 0 to 127, as said below
- gate_proj: bfloat16 [4, 8, 4096, 384], P('section', 'expert'), may hold values from -0.09375 to 0.09375
- up_proj: bfloat16 [4, 8, 4096, 384], P('section', 'expert'), may hold values from -0.09375 to 0.09375
- down_proj: bfloat16 [4, 8, 384, 4096], P('section', 'expert'), may hold values from -0.15625 to 0.15625
Outputs:
- passed: bfloat16 [4, 512, 4096], P('section', 'expert')
The draws below stay inside these ranges and needn't reach their ends.
Inputs may be any that keep to these rules, and one draw needn't show every extreme that they name: `expert_labels`: each row names 8 different experts, exactly one of them below 2. At most 56 of the 64 tokens of one device name one expert below 2, and on every device some expert is named by 56 of them. `cache_fill`: at least 128; some section has 256.
All inputs are finite; a program needn't handle non-finite values.
Results may differ from the reference program's by a relative error of at most 0.008.
Values may be sent and summed in bfloat16 or wider, within the bound.
A program may use at most 256 MiB of HBM per device.

```python
import math
import jax
import jax.numpy as jnp
from jax import lax

D = 4096
QUERY_HEADS = 32
KEY_VALUE_HEADS = 2
HEAD_SIZE = 128
EXPERTS = 128
TOPK = 8
FF = 1536
SPLIT = 4
TOK_DEV = 64
RELAY_SECTIONS = 4
EXPERTS_AIRBORNE = 2
FF_DEV = 384
CAP = 56
TOKENS = 512
CACHE = 256
N_EXPERT = 8


def draw_queries(key, part):
    key = jax.random.fold_in(key, 3)
    array_shape = (RELAY_SECTIONS, TOKENS, QUERY_HEADS * HEAD_SIZE)
    values = jnp.clip(jax.random.normal(key, array_shape, jnp.float32), -10.0, 10.0)
    return values.astype(jnp.bfloat16)


def key_value_pair(key, row_block):
    key_part, value_part = jax.random.split(key)
    array_shape = (RELAY_SECTIONS, 1, row_block, KEY_VALUE_HEADS * HEAD_SIZE)
    values = jnp.clip(jax.random.normal(value_part, array_shape, jnp.float32), -10.0, 10.0)
    keys_drawn = jnp.clip(jax.random.normal(key_part, array_shape, jnp.float32), -10.0, 10.0)
    return jnp.concatenate([keys_drawn, values], axis=1).astype(jnp.bfloat16)


def draw_fresh_kv(key, part):
    key = jax.random.fold_in(key, 5)
    return key_value_pair(key, TOKENS)


def draw_cache_kv(key, part):
    key = jax.random.fold_in(key, 7)
    return key_value_pair(key, CACHE)


def draw_cache_fill(key, part):
    key = jax.random.fold_in(key, 9)
    first, second = jax.random.split(key)
    fills = jax.random.randint(first, (RELAY_SECTIONS,), CACHE // 2, CACHE + 1)
    full_section = jax.random.randint(second, (), 0, RELAY_SECTIONS)
    return jnp.where(jnp.arange(RELAY_SECTIONS) == full_section, CACHE, fills).astype(jnp.int32)


def draw_router_weight(key, part):
    key = jax.random.fold_in(key, 13)
    array_shape = (RELAY_SECTIONS, D, EXPERTS)
    values = jnp.clip(jax.random.normal(key, array_shape, jnp.float32) / D ** 0.5, -3.0, 3.0)
    return values.astype(jnp.bfloat16)


def block_picks(key, hot_expert):
    order_key, others_key = jax.random.split(key)
    rank = jax.random.permutation(order_key, TOK_DEV)
    others = jax.random.permutation(others_key, EXPERTS_AIRBORNE - 1)
    other_pick = others[jnp.maximum(rank - CAP, 0) % (EXPERTS_AIRBORNE - 1)]
    other_pick = other_pick + (other_pick >= hot_expert).astype(jnp.int32)
    return jnp.where(rank < CAP, hot_expert, other_pick).astype(jnp.int32)


def token_vector(key, airborne_label):
    perm_key, roll_key = jax.random.split(key)
    outside_mask = jax.random.permutation(perm_key, EXPERTS - EXPERTS_AIRBORNE)[:TOPK - 1] + EXPERTS_AIRBORNE
    current_row = jnp.concatenate([airborne_label[None], outside_mask.astype(jnp.int32)])
    return jnp.roll(current_row, jax.random.randint(roll_key, (), 0, TOPK))


def draw_expert_labels(key, part):
    key = jax.random.fold_in(key, 11)
    hot_key, block_key, row_key = jax.random.split(key, 3)
    hot_experts = jax.random.randint(hot_key, (RELAY_SECTIONS,), 0, EXPERTS_AIRBORNE)
    cache_blocks = TOKENS // TOK_DEV
    block_keys = jax.random.split(block_key, RELAY_SECTIONS * cache_blocks)
    hot_each = jnp.repeat(hot_experts, cache_blocks)
    picks = jax.vmap(block_picks)(block_keys, hot_each).reshape(RELAY_SECTIONS * TOKENS)
    row_keys = jax.random.split(row_key, RELAY_SECTIONS * TOKENS)
    row_block = jax.vmap(token_vector)(row_keys, picks)
    return row_block.reshape(RELAY_SECTIONS, TOKENS, TOPK).astype(jnp.int32)


def block_levels(rng, dims, pieces, low, largest):
    def one(axis_at, parts):
        steps = jax.random.uniform(jax.random.fold_in(jax.random.fold_in(rng, 6), axis_at), (parts,), jnp.float32, low / len(pieces), largest / len(pieces))
        return jnp.repeat(jnp.exp(steps), dims[axis_at] // parts).reshape((-1,) + (1,) * (len(dims) - axis_at - 1))

    gain = one(*pieces[0])
    for cut in pieces[1:]:
        gain = gain * one(*cut)
    return gain


def centred(stream_key, shape, deviation, reach, cuts=(), kind=jnp.bfloat16):
    result = deviation * jax.random.normal(stream_key, shape, jnp.float32)
    if cuts:
        result = result * block_levels(stream_key, shape, cuts, -0.22, 0.18)
    return jnp.clip(result, -reach, reach).astype(kind)


def setup_inputs(seed: int = 0) -> dict:
    seeds = jax.random.split(jax.random.key(seed), 13)
    return {
        "hidden": centred(seeds[0], (RELAY_SECTIONS, TOKENS, D), 1.0, 6.0, ((0, 4), (1, 8))),
        "queries": draw_queries(jax.random.fold_in(seeds[12], 71), 0),
        "fresh_kv": draw_fresh_kv(jax.random.fold_in(seeds[12], 71), 0),
        "cache_kv": draw_cache_kv(jax.random.fold_in(seeds[12], 71), 0),
        "cache_fill": draw_cache_fill(jax.random.fold_in(seeds[12], 71), 0),
        "out_proj": centred(seeds[5], (RELAY_SECTIONS, QUERY_HEADS * HEAD_SIZE, D), (QUERY_HEADS * HEAD_SIZE // 16) ** -0.5, 0.375, ((0, 4), (1, 8))),
        "norm_gain": jnp.clip(1.0 + 0.1 * jax.random.normal(seeds[6], (RELAY_SECTIONS, D), jnp.float32), 0.5, 1.5).astype(jnp.bfloat16),
        "router_weight": draw_router_weight(jax.random.fold_in(seeds[12], 71), 0),
        "expert_labels": draw_expert_labels(jax.random.fold_in(seeds[12], 71), 0),
        "gate_proj": centred(seeds[9], (RELAY_SECTIONS, N_EXPERT, D, FF_DEV), D ** -0.5, 0.09375, ((0, 4), (1, 8))),
        "up_proj": centred(seeds[10], (RELAY_SECTIONS, N_EXPERT, D, FF_DEV), D ** -0.5, 0.09375, ((0, 4), (1, 8))),
        "down_proj": centred(seeds[11], (RELAY_SECTIONS, N_EXPERT, FF_DEV, D), FF ** -0.5, 0.15625, ((0, 4), (1, 8))),
    }


def attend_section(queries, fresh_kv, cache_kv, fill):
    cache_length = CACHE + TOKENS
    joined_rows = jnp.concatenate([cache_kv, fresh_kv], axis=1)
    gathered_keys = joined_rows[0].reshape(cache_length, KEY_VALUE_HEADS, HEAD_SIZE)
    gathered_values = joined_rows[1].reshape(cache_length, KEY_VALUE_HEADS, HEAD_SIZE)
    gathered_queries = queries.reshape(TOKENS, QUERY_HEADS, HEAD_SIZE)
    column = jnp.arange(cache_length, dtype=jnp.int32)[None, :]
    row_pos = jnp.arange(TOKENS, dtype=jnp.int32)[:, None]
    visible = jnp.where(column < CACHE, column < fill, column - CACHE <= row_pos)
    head_group = QUERY_HEADS // KEY_VALUE_HEADS
    scale = 1.0 / math.sqrt(HEAD_SIZE)

    def one_head(head):
        kv_head = head // head_group
        query_head = lax.dynamic_index_in_dim(gathered_queries, head, 1, keepdims=False)
        key_head = lax.dynamic_index_in_dim(gathered_keys, kv_head, 1, keepdims=False)
        value_head = lax.dynamic_index_in_dim(gathered_values, kv_head, 1, keepdims=False)
        scores = jnp.dot(query_head, key_head.T, preferred_element_type=jnp.float32) * scale
        masked = jnp.where(visible, scores, -1e+30)
        highest = lax.optimization_barrier(jnp.max(masked, axis=1, keepdims=True))
        weights = jnp.where(visible, jnp.exp(masked - highest), 0.0)
        totals = lax.optimization_barrier(jnp.sum(weights, axis=1, keepdims=True))
        rounded = weights.astype(jnp.bfloat16)
        return jnp.dot(rounded, value_head, preferred_element_type=jnp.float32) / totals
    heads_out = lax.map(one_head, jnp.arange(QUERY_HEADS, dtype=jnp.int32))
    return jnp.transpose(heads_out, (1, 0, 2)).reshape(TOKENS, QUERY_HEADS * HEAD_SIZE).astype(jnp.bfloat16)

def section_layer(hidden, queries, fresh_kv, cache_kv, fill, out_proj, norm_gain, router_weight, expert_labels, gate_proj, up_proj, down_proj):
    attended = attend_section(queries, fresh_kv, cache_kv, fill)
    projected = jnp.dot(attended, out_proj, preferred_element_type=jnp.float32)
    mixed = hidden.astype(jnp.float32) + projected
    inverse = lax.rsqrt(lax.optimization_barrier(jnp.mean(mixed * mixed, axis=1, keepdims=True)) + 1e-06)
    normed = (mixed * inverse * norm_gain.astype(jnp.float32)[None, :]).astype(jnp.bfloat16)
    logits = jnp.dot(normed, router_weight, preferred_element_type=jnp.float32)
    picked = jnp.take_along_axis(logits, expert_labels, axis=1)
    probabilities = jax.nn.softmax(picked, axis=1)
    airborne_mask = expert_labels < EXPERTS_AIRBORNE
    selected_experts = lax.optimization_barrier(jnp.sum(jnp.where(airborne_mask, expert_labels, 0), axis=1)).astype(jnp.int32)
    merge_results = lax.optimization_barrier(jnp.sum(jnp.where(airborne_mask, probabilities, 0.0), axis=1))
    gate_full = jnp.transpose(gate_proj.reshape(EXPERTS_AIRBORNE, SPLIT, D, FF_DEV), (0, 2, 1, 3)).reshape(EXPERTS_AIRBORNE, D, FF)
    up_full = jnp.transpose(up_proj.reshape(EXPERTS_AIRBORNE, SPLIT, D, FF_DEV), (0, 2, 1, 3)).reshape(EXPERTS_AIRBORNE, D, FF)
    down_full = down_proj.reshape(EXPERTS_AIRBORNE, FF, D)
    most_rows = N_EXPERT * CAP

    def one_expert(expert):
        hits = selected_experts == expert
        members = jnp.nonzero(hits, size=most_rows, fill_value=0)[0].astype(jnp.int32)
        valid = jnp.arange(most_rows, dtype=jnp.int32) < jnp.sum(hits.astype(jnp.int32))
        row_block = normed[members]
        gate_mat = lax.dynamic_index_in_dim(gate_full, expert, 0, keepdims=False)
        up_mat = lax.dynamic_index_in_dim(up_full, expert, 0, keepdims=False)
        down_mat = lax.dynamic_index_in_dim(down_full, expert, 0, keepdims=False)
        gated = jnp.dot(row_block, gate_mat, preferred_element_type=jnp.float32)
        lifted = jnp.dot(row_block, up_mat, preferred_element_type=jnp.float32)
        activation = (jax.nn.silu(gated) * lifted).astype(jnp.bfloat16)
        output = jnp.dot(activation, down_mat, preferred_element_type=jnp.float32)
        return (jnp.where(valid[:, None], output, 0.0), members)
    outputs, members = lax.map(one_expert, jnp.arange(EXPERTS_AIRBORNE, dtype=jnp.int32))
    routed = jnp.zeros((TOKENS, D), jnp.float32).at[members.reshape(-1)].add(outputs.reshape(-1, D))
    return (mixed + merge_results[:, None] * routed).astype(jnp.bfloat16)

def reference(hidden, queries, fresh_kv, cache_kv, cache_fill, out_proj, norm_gain, router_weight, expert_labels, gate_proj, up_proj, down_proj):
    results = []
    for section in range(RELAY_SECTIONS):
        results.append(section_layer(hidden[section], queries[section], fresh_kv[section], cache_kv[section], cache_fill[section], out_proj[section], norm_gain[section], router_weight[section], expert_labels[section], gate_proj[section], up_proj[section], down_proj[section]))
    return jnp.stack([results[(section - 1) % RELAY_SECTIONS] for section in range(RELAY_SECTIONS)], axis=0)
```

```python
import math

import jax
import jax.numpy as jnp
from jax import lax
from jax.sharding import PartitionSpec as P

D = 4096
QUERY_HEADS = 32
KEY_VALUE_HEADS = 2
HEAD_SIZE = 128
EXPERTS = 128
SPLIT = 4


def shifted(shard, axis, by):
    length = lax.axis_size(axis)
    return lax.ppermute(shard, axis, [(i, (i + by) % length) for i in range(length)])


def shards(
    hidden,
    queries,
    fresh_kv,
    cache_kv,
    cache_fill,
    out_proj,
    norm_gain,
    router_weight,
    expert_labels,
    gate_proj,
    up_proj,
    down_proj,
):
    devices = lax.axis_size("expert")
    device_index = lax.axis_index("expert")
    section_tokens = hidden.shape[1]
    local_cache = cache_kv.shape[2]
    stride = local_cache + section_tokens
    head_group = QUERY_HEADS // KEY_VALUE_HEADS
    scale = 1.0 / math.sqrt(HEAD_SIZE)
    fill = cache_fill[0]
    query_pos = device_index * section_tokens + jnp.arange(section_tokens, dtype=jnp.int32)
    gathered_queries = queries[0].reshape(section_tokens, KEY_VALUE_HEADS, head_group, HEAD_SIZE)
    joined_rows = jnp.concatenate([cache_kv[0], fresh_kv[0]], axis=1)

    def attend_block(carry, block_key_value, start):
        run_max, run_sum, run_acc = carry
        token_count = block_key_value.shape[1]
        row_index = start + jnp.arange(token_count, dtype=jnp.int32)
        owner = row_index // stride
        offset = row_index % stride
        cache_pos = owner * local_cache + offset
        slice_pos = owner * section_tokens + offset - local_cache
        visible = jnp.where(
            offset[None, :] < local_cache,
            cache_pos[None, :] < fill,
            slice_pos[None, :] <= query_pos[:, None],
        )
        key_matrix = block_key_value[0].reshape(token_count, KEY_VALUE_HEADS, HEAD_SIZE)
        value_matrix = block_key_value[1].reshape(token_count, KEY_VALUE_HEADS, HEAD_SIZE)
        scores = (
            jnp.einsum(
                "tgkd,rgd->tgkr", gathered_queries, key_matrix, preferred_element_type=jnp.float32
            )
            * scale
        )
        mask = visible[:, None, None, :]
        masked = jnp.where(mask, scores, -1e30)
        new_max = jnp.maximum(run_max, jnp.max(masked, axis=3))
        weights = jnp.where(mask, jnp.exp(masked - new_max[..., None]), 0.0)
        factor = jnp.exp(run_max - new_max)
        new_sum = run_sum * factor + jnp.sum(weights, axis=3)
        rounded = weights.astype(jnp.bfloat16)
        new_acc = run_acc * factor[..., None] + jnp.einsum(
            "tgkr,rgd->tgkd", rounded, value_matrix, preferred_element_type=jnp.float32
        )
        return (new_max, new_sum, new_acc)

    def attend_piece(carry, piece, start):
        token_count = piece.shape[1]
        cache_block = token_count
        while cache_block > 1024 and cache_block % 2 == 0:
            cache_block = cache_block // 2
        relay_steps = token_count // cache_block
        if relay_steps == 1:
            return attend_block(carry, piece, start)
        cache_blocks = jnp.transpose(
            piece.reshape(2, relay_steps, cache_block, KEY_VALUE_HEADS * HEAD_SIZE), (1, 0, 2, 3)
        )
        offsets = start + jnp.arange(relay_steps, dtype=jnp.int32) * cache_block

        def one_step(state, item):
            block_key_value, first = item
            return (attend_block(state, block_key_value, first), None)

        final, unused = lax.scan(one_step, carry, (cache_blocks, offsets))
        return final

    initial_maximum = jnp.full((section_tokens, KEY_VALUE_HEADS, head_group), -1e30, jnp.float32)
    initial_sum = jnp.zeros((section_tokens, KEY_VALUE_HEADS, head_group), jnp.float32)
    initial_accumulator = jnp.zeros(
        (section_tokens, KEY_VALUE_HEADS, head_group, HEAD_SIZE), jnp.float32
    )
    every_key_value = lax.all_gather(joined_rows, "expert", axis=1, tiled=True)
    final_max, final_sum, final_acc = attend_piece(
        (initial_maximum, initial_sum, initial_accumulator), every_key_value, jnp.int32(0)
    )
    attended = (
        (final_acc / final_sum[..., None])
        .reshape(section_tokens, QUERY_HEADS * HEAD_SIZE)
        .astype(jnp.bfloat16)
    )
    features = lax.all_to_all(attended, "expert", split_axis=1, concat_axis=0, tiled=True)
    partial_projected = jnp.dot(features, out_proj[0], preferred_element_type=jnp.float32)
    projected = lax.psum_scatter(
        partial_projected.astype(jnp.bfloat16), "expert", scatter_dimension=0, tiled=True
    ).astype(jnp.float32)
    mixed = hidden[0].astype(jnp.float32) + projected
    inverse = lax.rsqrt(jnp.mean(mixed * mixed, axis=1, keepdims=True) + 1e-06)
    normed = (mixed * inverse * norm_gain[0].astype(jnp.float32)[None, :]).astype(jnp.bfloat16)
    logits = jnp.dot(normed, router_weight[0], preferred_element_type=jnp.float32)
    label_rows = expert_labels[0]
    matches = label_rows[:, :, None] == jnp.arange(EXPERTS, dtype=jnp.int32)[None, None, :]
    picked = jnp.sum(jnp.where(matches, logits[:, None, :], 0.0), axis=2)
    probabilities = jax.nn.softmax(picked, axis=1)
    airborne_expert = devices // SPLIT
    hot_rows = SPLIT * max(1, section_tokens // (8 * SPLIT))
    other_rows = (section_tokens - hot_rows + airborne_expert - 2) // (airborne_expert - 1)
    capacity = SPLIT * ((max(hot_rows, other_rows) + SPLIT - 1) // SPLIT)
    airborne_mask = label_rows < airborne_expert
    selected_experts = jnp.sum(jnp.where(airborne_mask, label_rows, 0), axis=1)
    merge_results = jnp.sum(jnp.where(airborne_mask, probabilities, 0.0), axis=1)
    member = (
        selected_experts[:, None] == jnp.arange(airborne_expert, dtype=jnp.int32)[None, :]
    ).astype(jnp.int32)
    earlier = jnp.cumsum(member, axis=0) - member
    slot = jnp.sum(earlier * member, axis=1)
    code = selected_experts * capacity + slot
    table = (
        code[None, :] == jnp.arange(airborne_expert * capacity, dtype=jnp.int32)[:, None]
    ).astype(jnp.bfloat16)
    packed = (
        jnp.dot(table, normed, preferred_element_type=jnp.float32)
        .astype(jnp.bfloat16)
        .reshape(airborne_expert, capacity, D)
    )
    outgoing = jnp.repeat(packed, SPLIT, axis=0)
    received = lax.all_to_all(outgoing, "expert", split_axis=0, concat_axis=0, tiled=True)
    row_block = received.reshape(devices * capacity, D)
    gated = jnp.dot(row_block, gate_proj[0, 0], preferred_element_type=jnp.float32)
    lifted = jnp.dot(row_block, up_proj[0, 0], preferred_element_type=jnp.float32)
    activation = (jax.nn.silu(gated) * lifted).astype(jnp.bfloat16)
    partial_value = jnp.dot(
        activation, down_proj[0, 0], preferred_element_type=jnp.float32
    ).reshape(devices, capacity, D)
    returned = lax.all_to_all(
        partial_value.astype(jnp.bfloat16), "expert", split_axis=0, concat_axis=0, tiled=True
    ).astype(partial_value.dtype)
    summed = jnp.sum(returned.reshape(airborne_expert, SPLIT, capacity, D), axis=1).reshape(
        airborne_expert * capacity, D
    )
    routed = summed[code]
    result = (mixed + merge_results[:, None] * routed).astype(jnp.bfloat16)
    return shifted(result[None], "section", 1)


def solution(mesh):
    in_specs = (
        P("section", "expert", None),
        P("section", "expert", None),
        P("section", None, "expert", None),
        P("section", None, "expert", None),
        P("section"),
        P("section", "expert", None),
        P("section", None),
        P("section", None, None),
        P("section", "expert", None),
        P("section", "expert", None, None),
        P("section", "expert", None, None),
        P("section", "expert", None, None),
    )
    out_specs = P("section", "expert", None)
    return jax.shard_map(shards, mesh=mesh, in_specs=in_specs, out_specs=out_specs, check_vma=False)
```

```python
import functools
import math

import jax
import jax.numpy as jnp
from jax import lax
from jax.experimental import pallas as pl
from jax.experimental.pallas import tpu as pltpu
from jax.sharding import PartitionSpec as P

D = 4096
QUERY_HEADS = 32
KEY_VALUE_HEADS = 2
HEAD_SIZE = 128
EXPERTS = 128
SPLIT = 4


def shifted(shard, axis, by):
    length = lax.axis_size(axis)
    return lax.ppermute(shard, axis, [(i, (i + by) % length) for i in range(length)])


def shards(
    hidden,
    queries,
    fresh_kv,
    cache_kv,
    cache_fill,
    out_proj,
    norm_gain,
    router_weight,
    expert_labels,
    gate_proj,
    up_proj,
    down_proj,
):
    devices = lax.axis_size("expert")
    device_index = lax.axis_index("expert")
    section_tokens = hidden.shape[1]
    local_cache = cache_kv.shape[2]
    stride = local_cache + section_tokens
    head_group = QUERY_HEADS // KEY_VALUE_HEADS
    scale = 1.0 / math.sqrt(HEAD_SIZE)
    fill = cache_fill[0]
    query_pos = device_index * section_tokens + jnp.arange(section_tokens, dtype=jnp.int32)
    gathered_queries = queries[0].reshape(section_tokens, KEY_VALUE_HEADS, head_group, HEAD_SIZE)
    joined_rows = jnp.concatenate([cache_kv[0], fresh_kv[0]], axis=1)

    def attend_block(carry, block_key_value, start):
        run_max, run_sum, run_acc = carry
        token_count = block_key_value.shape[1]
        row_index = start + jnp.arange(token_count, dtype=jnp.int32)
        owner = row_index // stride
        offset = row_index % stride
        cache_pos = owner * local_cache + offset
        slice_pos = owner * section_tokens + offset - local_cache
        visible = jnp.where(
            offset[None, :] < local_cache,
            cache_pos[None, :] < fill,
            slice_pos[None, :] <= query_pos[:, None],
        )
        key_matrix = block_key_value[0].reshape(token_count, KEY_VALUE_HEADS, HEAD_SIZE)
        value_matrix = block_key_value[1].reshape(token_count, KEY_VALUE_HEADS, HEAD_SIZE)
        scores = (
            jnp.einsum(
                "tgkd,rgd->tgkr", gathered_queries, key_matrix, preferred_element_type=jnp.float32
            )
            * scale
        )
        mask = visible[:, None, None, :]
        masked = jnp.where(mask, scores, -1e30)
        new_max = jnp.maximum(run_max, jnp.max(masked, axis=3))
        weights = jnp.where(mask, jnp.exp(masked - new_max[..., None]), 0.0)
        factor = jnp.exp(run_max - new_max)
        new_sum = run_sum * factor + jnp.sum(weights, axis=3)
        rounded = weights.astype(jnp.bfloat16)
        new_acc = run_acc * factor[..., None] + jnp.einsum(
            "tgkr,rgd->tgkd", rounded, value_matrix, preferred_element_type=jnp.float32
        )
        return (new_max, new_sum, new_acc)

    def attend_piece(carry, piece, start):
        token_count = piece.shape[1]
        cache_block = token_count
        while cache_block > 1024 and cache_block % 2 == 0:
            cache_block = cache_block // 2
        relay_steps = token_count // cache_block
        if relay_steps == 1:
            return attend_block(carry, piece, start)
        cache_blocks = jnp.transpose(
            piece.reshape(2, relay_steps, cache_block, KEY_VALUE_HEADS * HEAD_SIZE), (1, 0, 2, 3)
        )
        offsets = start + jnp.arange(relay_steps, dtype=jnp.int32) * cache_block

        def one_step(state, item):
            block_key_value, first = item
            return (attend_block(state, block_key_value, first), None)

        final, unused = lax.scan(one_step, carry, (cache_blocks, offsets))
        return final

    initial_maximum = jnp.full((section_tokens, KEY_VALUE_HEADS, head_group), -1e30, jnp.float32)
    initial_sum = jnp.zeros((section_tokens, KEY_VALUE_HEADS, head_group), jnp.float32)
    initial_accumulator = jnp.zeros(
        (section_tokens, KEY_VALUE_HEADS, head_group, HEAD_SIZE), jnp.float32
    )
    every_key_value = lax.all_gather(joined_rows, "expert", axis=1, tiled=True)
    final_max, final_sum, final_acc = attend_piece(
        (initial_maximum, initial_sum, initial_accumulator), every_key_value, jnp.int32(0)
    )
    attended = (
        (final_acc / final_sum[..., None])
        .reshape(section_tokens, QUERY_HEADS * HEAD_SIZE)
        .astype(jnp.bfloat16)
    )
    features = lax.all_to_all(attended, "expert", split_axis=1, concat_axis=0, tiled=True)
    partial_projected = jnp.dot(features, out_proj[0], preferred_element_type=jnp.float32)
    projected = lax.psum_scatter(
        partial_projected.astype(jnp.bfloat16), "expert", scatter_dimension=0, tiled=True
    ).astype(jnp.float32)
    mixed = hidden[0].astype(jnp.float32) + projected
    inverse = lax.rsqrt(jnp.mean(mixed * mixed, axis=1, keepdims=True) + 1e-06)
    normed = (mixed * inverse * norm_gain[0].astype(jnp.float32)[None, :]).astype(jnp.bfloat16)
    logits = jnp.dot(normed, router_weight[0], preferred_element_type=jnp.float32)
    label_rows = expert_labels[0]
    matches = label_rows[:, :, None] == jnp.arange(EXPERTS, dtype=jnp.int32)[None, None, :]
    picked = jnp.sum(jnp.where(matches, logits[:, None, :], 0.0), axis=2)
    probabilities = jax.nn.softmax(picked, axis=1)
    airborne_expert = devices // SPLIT
    hot_rows = SPLIT * max(1, section_tokens // (8 * SPLIT))
    other_rows = (section_tokens - hot_rows + airborne_expert - 2) // (airborne_expert - 1)
    capacity = SPLIT * ((max(hot_rows, other_rows) + SPLIT - 1) // SPLIT)
    airborne_mask = label_rows < airborne_expert
    selected_experts = jnp.sum(jnp.where(airborne_mask, label_rows, 0), axis=1)
    merge_results = jnp.sum(jnp.where(airborne_mask, probabilities, 0.0), axis=1)
    member = (
        selected_experts[:, None] == jnp.arange(airborne_expert, dtype=jnp.int32)[None, :]
    ).astype(jnp.int32)
    earlier = jnp.cumsum(member, axis=0) - member
    slot = jnp.sum(earlier * member, axis=1)
    code = selected_experts * capacity + slot
    table = (
        code[None, :] == jnp.arange(airborne_expert * capacity, dtype=jnp.int32)[:, None]
    ).astype(jnp.bfloat16)
    packed = (
        jnp.dot(table, normed, preferred_element_type=jnp.float32)
        .astype(jnp.bfloat16)
        .reshape(airborne_expert, capacity, D)
    )
    outgoing = jnp.repeat(packed, SPLIT, axis=0)
    received = lax.all_to_all(outgoing, "expert", split_axis=0, concat_axis=0, tiled=True)
    row_block = received.reshape(devices * capacity, D)
    gated = jnp.dot(row_block, gate_proj[0, 0], preferred_element_type=jnp.float32)
    lifted = jnp.dot(row_block, up_proj[0, 0], preferred_element_type=jnp.float32)
    activation = (jax.nn.silu(gated) * lifted).astype(jnp.bfloat16)
    partial_value = jnp.dot(
        activation, down_proj[0, 0], preferred_element_type=jnp.float32
    ).reshape(devices, capacity, D)
    returned = lax.all_to_all(
        partial_value.astype(jnp.bfloat16), "expert", split_axis=0, concat_axis=0, tiled=True
    ).astype(partial_value.dtype)
    summed = jnp.sum(returned.reshape(airborne_expert, SPLIT, capacity, D), axis=1).reshape(
        airborne_expert * capacity, D
    )
    routed = summed[code]
    result = (mixed + merge_results[:, None] * routed).astype(jnp.bfloat16)
    return shifted(result[None], "section", 1)


MESH = pl.DeviceIdType.MESH
PIECES = 4


def tick_kernel(
    sizes,
    query_ref,
    rows_ref,
    hidden_ref,
    fill_ref,
    gain_ref,
    label_ref,
    out_proj_hbm,
    router_hbm,
    gate_hbm,
    up_hbm,
    down_hbm,
    out_ref,
    out_proj_ref,
    router_ref,
    gate_ref,
    up_ref,
    down_ref,
    query_all,
    rows_all,
    keys_ref,
    values_ref,
    attended_ref,
    pair_send,
    pair_recv,
    part_ref,
    right_send,
    right_recv,
    left_send,
    left_recv,
    normed_ref,
    mixed_ref,
    combine_ref,
    expert_send,
    expert_recv,
    routed_ref,
    back_right_send,
    back_right_recv,
    back_left_send,
    back_left_recv,
    result_ref,
    weight_sem,
    query_send_sem,
    query_recv_sem,
    rows_send_sem,
    rows_recv_sem,
    share_send_sem,
    share_recv_sem,
    pair_sem,
    right_sem,
    left_sem,
    norm_sem,
    expert_sem,
    back_right_sem,
    back_left_sem,
    out_sem,
):
    devices, sections, tokens, cache_rows, heads, head_group, local_experts = sizes
    chips = devices // 2
    width = hidden_ref.shape[1] // PIECES
    section = lax.axis_index("section")
    me = lax.axis_index("expert")
    chip, core = me // 2, me % 2
    partner = me + 1 - 2 * core
    next_section = (section + 1) % sections
    before_section = (section + sections - 1) % sections
    right = (me + 2) % devices
    left = (me + devices - 2) % devices

    def remote(source, target, send_sem, recv_sem, to, to_section=None):
        return pltpu.make_async_remote_copy(
            src_ref=source,
            dst_ref=target,
            send_sem=send_sem,
            recv_sem=recv_sem,
            device_id=(section if to_section is None else to_section, to),
            device_id_type=MESH,
        )

    weights = [
        pltpu.make_async_copy(source, target, weight_sem.at[at])
        for at, (source, target) in enumerate(
            [
                (out_proj_hbm, out_proj_ref),
                (gate_hbm, gate_ref),
                (up_hbm, up_ref),
                (down_hbm, down_ref),
                (router_hbm, router_ref),
            ]
        )
    ]

    barrier = pltpu.get_barrier_semaphore()
    for step in range(1, devices):
        pl.semaphore_signal(
            barrier, inc=1, device_id=(section, (me + step) % devices), device_id_type=MESH
        )
    pl.semaphore_signal(barrier, inc=1, device_id=(next_section, me), device_id_type=MESH)
    pl.semaphore_signal(barrier, inc=1, device_id=(before_section, me), device_id_type=MESH)
    pl.semaphore_wait(barrier, devices + 1)

    def key_head(chip_at):
        return (chip_at * 2 * heads) // head_group

    def query_copy(step):
        to = (me + step) % devices
        return remote(
            query_ref.at[to], query_all.at[me], query_send_sem.at[step], query_recv_sem.at[step], to
        )

    def rows_copy(step):
        to_chip = (chip + step) % chips
        return remote(
            rows_ref.at[key_head(to_chip)],
            rows_all.at[me],
            rows_send_sem.at[step],
            rows_recv_sem.at[step],
            2 * to_chip + core,
        )

    def share_copy(step):
        slot = 2 * ((chip + chips - step) % chips) + core
        return remote(
            rows_all.at[slot],
            rows_all.at[slot],
            share_send_sem.at[step],
            share_recv_sem.at[step],
            partner,
        )

    for step in range(1, chips):
        rows_copy(step).start()
    for step in range(1, devices):
        query_copy(step).start()
    for copy in weights:
        copy.start()
    query_all[me] = query_ref[me]
    rows_all[me] = rows_ref[key_head(chip)]
    for step in range(chips):
        if step > 0:
            rows_copy(step).wait_recv()
        share_copy(step).start()
    for step in range(chips):
        share_copy(step).wait_recv()

    for device in range(devices):
        at = 0
        for ref in (keys_ref, values_ref):
            start = devices * cache_rows + device * tokens
            ref[start : start + tokens] = rows_all[device, at : at + tokens]
            at += tokens
        for ref in (keys_ref, values_ref):
            start = device * cache_rows
            ref[start : start + cache_rows] = rows_all[device, at : at + cache_rows]
            at += cache_rows
    for step in range(1, devices):
        query_copy(step).wait_recv()
    weights[0].wait()

    fill = fill_ref[0]
    total_rows = keys_ref.shape[0]
    cached = devices * cache_rows
    group_rows = heads * tokens
    column = lax.broadcasted_iota(jnp.int32, (group_rows, total_rows), 1)
    row_token = lax.broadcasted_iota(jnp.int32, (group_rows, total_rows), 0) % tokens

    def home_of(step):
        return jnp.where(step % 2 == 0, step // 2, chips - 1 - step // 2)

    def pair_copy(step):
        return remote(
            pair_send.at[step], pair_recv.at[step], pair_sem.at[0, step], pair_sem.at[1, step], partner
        )

    def right_copy(step, piece):
        return remote(
            right_send.at[step, piece],
            right_recv.at[step, piece],
            right_sem.at[0, step, piece],
            right_sem.at[1, step, piece],
            right,
        )

    def left_copy(step, piece):
        return remote(
            left_send.at[step, piece],
            left_recv.at[step, piece],
            left_sem.at[0, step, piece],
            left_sem.at[1, step, piece],
            left,
        )

    def norm_copy(step):
        return remote(
            normed_ref.at[step, 0],
            normed_ref.at[step, 1],
            norm_sem.at[0, step],
            norm_sem.at[1, step],
            partner,
        )

    def expert_copy(step):
        return remote(
            expert_send.at[step],
            expert_recv.at[step],
            expert_sem.at[0, step],
            expert_sem.at[1, step],
            partner,
        )

    def back_right_copy(step, piece):
        return remote(
            back_right_send.at[step, piece],
            back_right_recv.at[step, piece],
            back_right_sem.at[0, step, piece],
            back_right_sem.at[1, step, piece],
            right,
        )

    def back_left_copy(step, piece):
        return remote(
            back_left_send.at[step, piece],
            back_left_recv.at[step, piece],
            back_left_sem.at[0, step, piece],
            back_left_sem.at[1, step, piece],
            left,
        )

    def out_copy(piece):
        return remote(
            result_ref.at[piece],
            out_ref.at[:, pl.ds(piece * width, width)],
            out_sem.at[0, piece],
            out_sem.at[1, piece],
            me,
            next_section,
        )

    def project(step, carry):
        home = home_of(step)
        for which in range(2):
            owner = 2 * home + (core if which == 0 else 1 - core)
            scores = (
                lax.dot_general(
                    query_all[owner],
                    keys_ref[...],
                    (((1,), (1,)), ((), ())),
                    preferred_element_type=jnp.float32,
                )
                * (1.0 / math.sqrt(HEAD_SIZE))
            )
            limit = jnp.where(column < cached, fill, cached + owner * tokens + row_token + 1)
            visible = column < limit
            masked = jnp.where(visible, scores, -1e30)
            highest = jnp.max(masked, axis=1, keepdims=True)
            weight = jnp.where(visible, jnp.exp(masked - highest), 0.0)
            totals = jnp.sum(weight, axis=1, keepdims=True)
            mean = (
                jnp.dot(
                    weight.astype(jnp.bfloat16), values_ref[...], preferred_element_type=jnp.float32
                )
                / totals
            ).astype(jnp.bfloat16)
            for head in range(heads):
                attended_ref[
                    which * tokens : (which + 1) * tokens, head * HEAD_SIZE : (head + 1) * HEAD_SIZE
                ] = mean[head * tokens : (head + 1) * tokens]
        for piece in range(PIECES):
            product = jnp.dot(
                attended_ref[...],
                out_proj_ref[:, piece * width : (piece + 1) * width],
                preferred_element_type=jnp.float32,
            )
            part_ref[step, piece] = product[:tokens]
            pair_send[step, piece] = product[tokens:].astype(jnp.bfloat16)
        pair_copy(step).start()

        @pl.when(home == chip)
        def _():
            for piece in range(PIECES):
                part_ref[step, piece] += hidden_ref[
                    :, piece * width : (piece + 1) * width
                ].astype(jnp.float32)

        pair_copy(step).wait_recv()
        for piece in range(PIECES):
            part_ref[step, piece] += pair_recv[step, piece].astype(jnp.float32)

            @pl.when(chip == 0)
            def _():
                right_send[step, piece] = part_ref[step, piece].astype(jnp.bfloat16)
                right_copy(step, piece).start()

            @pl.when(chip == chips - 1)
            def _():
                left_send[step, piece] = part_ref[step, piece].astype(jnp.bfloat16)
                left_copy(step, piece).start()

        return carry

    lax.fori_loop(0, chips, project, 0)
    for copy in weights[1:]:
        copy.wait()
    my_expert = (me // SPLIT).astype(jnp.float32)
    select_at = 2 * tokens + 2 * cache_rows

    def layer(step, carry):
        home = home_of(step)
        for piece in range(PIECES):

            @pl.when(chip > 0)
            def _():
                right_copy(step, piece).wait_recv()

                @pl.when(chip < chips - 1)
                def _():
                    right_send[step, piece] = (
                        part_ref[step, piece] + right_recv[step, piece].astype(jnp.float32)
                    ).astype(jnp.bfloat16)
                    right_copy(step, piece).start()

            @pl.when(chip < chips - 1)
            def _():
                left_copy(step, piece).wait_recv()

                @pl.when(chip > 0)
                def _():
                    left_send[step, piece] = (
                        part_ref[step, piece] + left_recv[step, piece].astype(jnp.float32)
                    ).astype(jnp.bfloat16)
                    left_copy(step, piece).start()

            @pl.when(chip > 0)
            def _():
                part_ref[step, piece] += right_recv[step, piece].astype(jnp.float32)

            @pl.when(chip < chips - 1)
            def _():
                part_ref[step, piece] += left_recv[step, piece].astype(jnp.float32)

        squares = jnp.zeros((tokens, 1), jnp.float32)
        for piece in range(PIECES):
            mixed = part_ref[step, piece]
            squares += jnp.sum(mixed * mixed, axis=1, keepdims=True)
        inverse = lax.rsqrt(squares / (PIECES * width) + 1e-06)
        for piece in range(PIECES):
            columns = slice(piece * width, (piece + 1) * width)
            normed_ref[step, 0, :, columns] = (
                part_ref[step, piece] * inverse * gain_ref[:, columns].astype(jnp.float32)
            ).astype(jnp.bfloat16)
        norm_copy(step).start()

        @pl.when(home == chip)
        def _():
            for piece in range(PIECES):
                mixed_ref[piece] = part_ref[step, piece]
            logits = jnp.dot(
                normed_ref[step, 0], router_ref[...], preferred_element_type=jnp.float32
            )
            labels = label_ref[...]
            expert_at = lax.broadcasted_iota(jnp.int32, logits.shape, 1)
            picked = []
            for at in range(labels.shape[1]):
                match = labels[:, at : at + 1] == expert_at
                picked.append(jnp.sum(jnp.where(match, logits, 0.0), axis=1, keepdims=True))
            highest = picked[0]
            for value in picked[1:]:
                highest = jnp.maximum(highest, value)
            total = jnp.zeros_like(highest)
            chosen = jnp.zeros_like(highest)
            for at, value in enumerate(picked):
                weight = jnp.exp(value - highest)
                total += weight
                chosen += jnp.where(labels[:, at : at + 1] < local_experts, weight, 0.0)
            combine_ref[...] = jnp.broadcast_to(chosen / total, combine_ref.shape)

        norm_copy(step).wait_recv()
        rows = normed_ref[step].reshape(2 * tokens, PIECES * width)
        gated = jnp.dot(rows, gate_ref[...], preferred_element_type=jnp.float32)
        lifted = jnp.dot(rows, up_ref[...], preferred_element_type=jnp.float32)
        activation = gated / (1.0 + jnp.exp(-gated)) * lifted
        selected = jnp.concatenate(
            [
                rows_all[2 * home + core, select_at : select_at + tokens],
                rows_all[2 * home + 1 - core, select_at : select_at + tokens],
            ],
            axis=0,
        ).astype(jnp.float32)[:, :1]
        activation = jnp.where(selected == my_expert, activation, 0.0).astype(jnp.bfloat16)
        for piece in range(PIECES):
            product = jnp.dot(
                activation,
                down_ref[:, piece * width : (piece + 1) * width],
                preferred_element_type=jnp.float32,
            )
            routed_ref[step, piece] = product[:tokens]
            expert_send[step, piece] = product[tokens:].astype(jnp.bfloat16)
        expert_copy(step).start()
        expert_copy(step).wait_recv()
        for piece in range(PIECES):
            routed_ref[step, piece] += expert_recv[step, piece].astype(jnp.float32)

            @pl.when((chip == 0) & (home > 0))
            def _():
                back_right_send[step, piece] = routed_ref[step, piece].astype(jnp.bfloat16)
                back_right_copy(step, piece).start()

            @pl.when((chip == chips - 1) & (home < chips - 1))
            def _():
                back_left_send[step, piece] = routed_ref[step, piece].astype(jnp.bfloat16)
                back_left_copy(step, piece).start()

        return carry

    lax.fori_loop(0, chips, layer, 0)

    def back(step, carry):
        home = home_of(step)
        for piece in range(PIECES):

            @pl.when((chip > 0) & (chip <= home))
            def _():
                back_right_copy(step, piece).wait_recv()
                routed_ref[step, piece] += back_right_recv[step, piece].astype(jnp.float32)

            @pl.when((chip > 0) & (chip < home))
            def _():
                back_right_send[step, piece] = routed_ref[step, piece].astype(jnp.bfloat16)
                back_right_copy(step, piece).start()

            @pl.when((chip < chips - 1) & (chip >= home))
            def _():
                back_left_copy(step, piece).wait_recv()
                routed_ref[step, piece] += back_left_recv[step, piece].astype(jnp.float32)

            @pl.when((chip < chips - 1) & (chip > home))
            def _():
                back_left_send[step, piece] = routed_ref[step, piece].astype(jnp.bfloat16)
                back_left_copy(step, piece).start()

            @pl.when(chip == home)
            def _():
                result_ref[piece] = (
                    mixed_ref[piece] + combine_ref[:, :1] * routed_ref[step, piece]
                ).astype(jnp.bfloat16)
                out_copy(piece).start()

        return carry

    lax.fori_loop(0, chips, back, 0)

    def drain(step, carry):
        home = home_of(step)
        pair_copy(step).wait_send()
        norm_copy(step).wait_send()
        expert_copy(step).wait_send()
        for piece in range(PIECES):

            @pl.when(chip < chips - 1)
            def _():
                right_copy(step, piece).wait_send()

            @pl.when(chip > 0)
            def _():
                left_copy(step, piece).wait_send()

            @pl.when(chip < home)
            def _():
                back_right_copy(step, piece).wait_send()

            @pl.when(chip > home)
            def _():
                back_left_copy(step, piece).wait_send()

        return carry

    lax.fori_loop(0, chips, drain, 0)
    for step in range(1, chips):
        rows_copy(step).wait_send()
    for step in range(chips):
        share_copy(step).wait_send()
    for step in range(1, devices):
        query_copy(step).wait_send()
    for piece in range(PIECES):
        out_copy(piece).wait()


def fused_shards(
    sections,
    hidden,
    queries,
    fresh_kv,
    cache_kv,
    cache_fill,
    out_proj,
    norm_gain,
    router_weight,
    expert_labels,
    gate_proj,
    up_proj,
    down_proj,
):
    devices = lax.axis_size("expert")
    chips = devices // 2
    tokens, model = hidden.shape[1:]
    cache_rows = cache_kv.shape[2]
    heads = QUERY_HEADS // devices
    head_group = QUERY_HEADS // KEY_VALUE_HEADS
    local_experts = devices // SPLIT
    features = heads * HEAD_SIZE
    hidden_units = gate_proj.shape[3]
    width = model // PIECES
    query_rows = jnp.transpose(
        queries[0].reshape(tokens, devices, heads, HEAD_SIZE), (1, 2, 0, 3)
    ).reshape(devices, heads * tokens, HEAD_SIZE)
    labels = expert_labels[0]
    selected = jnp.sum(jnp.where(labels < local_experts, labels, 0), axis=1)

    def by_head(array, length):
        return jnp.transpose(
            array.reshape(2, length, KEY_VALUE_HEADS, HEAD_SIZE), (2, 0, 1, 3)
        ).reshape(KEY_VALUE_HEADS, 2 * length, HEAD_SIZE)

    key_rows = jnp.concatenate(
        [
            by_head(fresh_kv[0], tokens),
            by_head(cache_kv[0], cache_rows),
            jnp.broadcast_to(
                selected.astype(jnp.bfloat16)[None, :, None], (KEY_VALUE_HEADS, tokens, HEAD_SIZE)
            ),
        ],
        axis=1,
    )
    message = key_rows.shape[1]
    bf16, f32 = jnp.bfloat16, jnp.float32
    vmem = pl.BlockSpec(memory_space=pltpu.VMEM)
    anywhere = pl.BlockSpec(memory_space=pl.ANY)
    block = (chips, PIECES, tokens, width)
    dma = pltpu.SemaphoreType.DMA
    sizes = (devices, sections, tokens, cache_rows, heads, head_group, local_experts)
    total_rows = devices * (tokens + cache_rows)
    result = pl.pallas_call(
        functools.partial(tick_kernel, sizes),
        out_shape=jax.ShapeDtypeStruct((tokens, model), bf16),
        in_specs=[vmem, vmem, vmem, pl.BlockSpec(memory_space=pltpu.SMEM), vmem, vmem]
        + [anywhere] * 5,
        out_specs=vmem,
        scratch_shapes=[
            pltpu.VMEM((features, model), bf16),
            pltpu.VMEM(router_weight.shape[1:], bf16),
            pltpu.VMEM((model, hidden_units), bf16),
            pltpu.VMEM((model, hidden_units), bf16),
            pltpu.VMEM((hidden_units, model), bf16),
            pltpu.VMEM((devices, heads * tokens, HEAD_SIZE), bf16),
            pltpu.VMEM((devices, message, HEAD_SIZE), bf16),
            pltpu.VMEM((total_rows, HEAD_SIZE), bf16),
            pltpu.VMEM((total_rows, HEAD_SIZE), bf16),
            pltpu.VMEM((2 * tokens, features), bf16),
            pltpu.VMEM(block, bf16),
            pltpu.VMEM(block, bf16),
            pltpu.VMEM(block, f32),
            pltpu.VMEM(block, bf16),
            pltpu.VMEM(block, bf16),
            pltpu.VMEM(block, bf16),
            pltpu.VMEM(block, bf16),
            pltpu.VMEM((chips, 2, tokens, model), bf16),
            pltpu.VMEM((PIECES, tokens, width), f32),
            pltpu.VMEM((tokens, 128), f32),
            pltpu.VMEM(block, bf16),
            pltpu.VMEM(block, bf16),
            pltpu.VMEM(block, f32),
            pltpu.VMEM(block, bf16),
            pltpu.VMEM(block, bf16),
            pltpu.VMEM(block, bf16),
            pltpu.VMEM(block, bf16),
            pltpu.VMEM((PIECES, tokens, width), bf16),
            dma((5,)),
            dma((devices,)),
            dma((devices,)),
            dma((chips,)),
            dma((chips,)),
            dma((chips,)),
            dma((chips,)),
            dma((2, chips)),
            dma((2, chips, PIECES)),
            dma((2, chips, PIECES)),
            dma((2, chips)),
            dma((2, chips)),
            dma((2, chips, PIECES)),
            dma((2, chips, PIECES)),
            dma((2, PIECES)),
        ],
        compiler_params=pltpu.CompilerParams(
            collective_id=0, has_side_effects=True, vmem_limit_bytes=60 * 2**20
        ),
    )(
        query_rows,
        key_rows,
        hidden[0],
        cache_fill,
        norm_gain,
        labels,
        out_proj[0],
        router_weight[0],
        gate_proj[0, 0],
        up_proj[0, 0],
        down_proj[0, 0],
    )
    return result[None]


def fits_one_kernel(mesh):
    devices = mesh.shape["expert"]
    if devices % 2 or QUERY_HEADS % devices:
        return False
    return (QUERY_HEADS // KEY_VALUE_HEADS) % (2 * (QUERY_HEADS // devices)) == 0


def solution(mesh):
    in_specs = (
        P("section", "expert", None),
        P("section", "expert", None),
        P("section", None, "expert", None),
        P("section", None, "expert", None),
        P("section"),
        P("section", "expert", None),
        P("section", None),
        P("section", None, None),
        P("section", "expert", None),
        P("section", "expert", None, None),
        P("section", "expert", None, None),
        P("section", "expert", None, None),
    )
    out_specs = P("section", "expert", None)
    body = shards
    if fits_one_kernel(mesh):
        body = functools.partial(fused_shards, mesh.shape["section"])
    return jax.shard_map(body, mesh=mesh, in_specs=in_specs, out_specs=out_specs, check_vma=False)
```

```python
import functools
import math

import jax
import jax.numpy as jnp
from jax import lax
from jax.experimental import pallas as pl
from jax.experimental.pallas import tpu as pltpu
from jax.sharding import PartitionSpec as P

D = 4096
QUERY_HEADS = 32
KEY_VALUE_HEADS = 2
HEAD_SIZE = 128
EXPERTS = 128
SPLIT = 4


def shifted(shard, axis, by):
    length = lax.axis_size(axis)
    return lax.ppermute(shard, axis, [(i, (i + by) % length) for i in range(length)])


def shards(
    hidden,
    queries,
    fresh_kv,
    cache_kv,
    cache_fill,
    out_proj,
    norm_gain,
    router_weight,
    expert_labels,
    gate_proj,
    up_proj,
    down_proj,
):
    devices = lax.axis_size("expert")
    device_index = lax.axis_index("expert")
    section_tokens = hidden.shape[1]
    local_cache = cache_kv.shape[2]
    stride = local_cache + section_tokens
    head_group = QUERY_HEADS // KEY_VALUE_HEADS
    scale = 1.0 / math.sqrt(HEAD_SIZE)
    fill = cache_fill[0]
    query_pos = device_index * section_tokens + jnp.arange(section_tokens, dtype=jnp.int32)
    gathered_queries = queries[0].reshape(section_tokens, KEY_VALUE_HEADS, head_group, HEAD_SIZE)
    joined_rows = jnp.concatenate([cache_kv[0], fresh_kv[0]], axis=1)

    def attend_block(carry, block_key_value, start):
        run_max, run_sum, run_acc = carry
        token_count = block_key_value.shape[1]
        row_index = start + jnp.arange(token_count, dtype=jnp.int32)
        owner = row_index // stride
        offset = row_index % stride
        cache_pos = owner * local_cache + offset
        slice_pos = owner * section_tokens + offset - local_cache
        visible = jnp.where(
            offset[None, :] < local_cache,
            cache_pos[None, :] < fill,
            slice_pos[None, :] <= query_pos[:, None],
        )
        key_matrix = block_key_value[0].reshape(token_count, KEY_VALUE_HEADS, HEAD_SIZE)
        value_matrix = block_key_value[1].reshape(token_count, KEY_VALUE_HEADS, HEAD_SIZE)
        scores = (
            jnp.einsum(
                "tgkd,rgd->tgkr", gathered_queries, key_matrix, preferred_element_type=jnp.float32
            )
            * scale
        )
        mask = visible[:, None, None, :]
        masked = jnp.where(mask, scores, -1e30)
        new_max = jnp.maximum(run_max, jnp.max(masked, axis=3))
        weights = jnp.where(mask, jnp.exp(masked - new_max[..., None]), 0.0)
        factor = jnp.exp(run_max - new_max)
        new_sum = run_sum * factor + jnp.sum(weights, axis=3)
        rounded = weights.astype(jnp.bfloat16)
        new_acc = run_acc * factor[..., None] + jnp.einsum(
            "tgkr,rgd->tgkd", rounded, value_matrix, preferred_element_type=jnp.float32
        )
        return (new_max, new_sum, new_acc)

    def attend_piece(carry, piece, start):
        token_count = piece.shape[1]
        cache_block = token_count
        while cache_block > 1024 and cache_block % 2 == 0:
            cache_block = cache_block // 2
        relay_steps = token_count // cache_block
        if relay_steps == 1:
            return attend_block(carry, piece, start)
        cache_blocks = jnp.transpose(
            piece.reshape(2, relay_steps, cache_block, KEY_VALUE_HEADS * HEAD_SIZE), (1, 0, 2, 3)
        )
        offsets = start + jnp.arange(relay_steps, dtype=jnp.int32) * cache_block

        def one_step(state, item):
            block_key_value, first = item
            return (attend_block(state, block_key_value, first), None)

        final, unused = lax.scan(one_step, carry, (cache_blocks, offsets))
        return final

    initial_maximum = jnp.full((section_tokens, KEY_VALUE_HEADS, head_group), -1e30, jnp.float32)
    initial_sum = jnp.zeros((section_tokens, KEY_VALUE_HEADS, head_group), jnp.float32)
    initial_accumulator = jnp.zeros(
        (section_tokens, KEY_VALUE_HEADS, head_group, HEAD_SIZE), jnp.float32
    )
    every_key_value = lax.all_gather(joined_rows, "expert", axis=1, tiled=True)
    final_max, final_sum, final_acc = attend_piece(
        (initial_maximum, initial_sum, initial_accumulator), every_key_value, jnp.int32(0)
    )
    attended = (
        (final_acc / final_sum[..., None])
        .reshape(section_tokens, QUERY_HEADS * HEAD_SIZE)
        .astype(jnp.bfloat16)
    )
    features = lax.all_to_all(attended, "expert", split_axis=1, concat_axis=0, tiled=True)
    partial_projected = jnp.dot(features, out_proj[0], preferred_element_type=jnp.float32)
    projected = lax.psum_scatter(
        partial_projected.astype(jnp.bfloat16), "expert", scatter_dimension=0, tiled=True
    ).astype(jnp.float32)
    mixed = hidden[0].astype(jnp.float32) + projected
    inverse = lax.rsqrt(jnp.mean(mixed * mixed, axis=1, keepdims=True) + 1e-06)
    normed = (mixed * inverse * norm_gain[0].astype(jnp.float32)[None, :]).astype(jnp.bfloat16)
    logits = jnp.dot(normed, router_weight[0], preferred_element_type=jnp.float32)
    label_rows = expert_labels[0]
    matches = label_rows[:, :, None] == jnp.arange(EXPERTS, dtype=jnp.int32)[None, None, :]
    picked = jnp.sum(jnp.where(matches, logits[:, None, :], 0.0), axis=2)
    probabilities = jax.nn.softmax(picked, axis=1)
    airborne_expert = devices // SPLIT
    hot_rows = SPLIT * max(1, section_tokens // (8 * SPLIT))
    other_rows = (section_tokens - hot_rows + airborne_expert - 2) // (airborne_expert - 1)
    capacity = SPLIT * ((max(hot_rows, other_rows) + SPLIT - 1) // SPLIT)
    airborne_mask = label_rows < airborne_expert
    selected_experts = jnp.sum(jnp.where(airborne_mask, label_rows, 0), axis=1)
    merge_results = jnp.sum(jnp.where(airborne_mask, probabilities, 0.0), axis=1)
    member = (
        selected_experts[:, None] == jnp.arange(airborne_expert, dtype=jnp.int32)[None, :]
    ).astype(jnp.int32)
    earlier = jnp.cumsum(member, axis=0) - member
    slot = jnp.sum(earlier * member, axis=1)
    code = selected_experts * capacity + slot
    table = (
        code[None, :] == jnp.arange(airborne_expert * capacity, dtype=jnp.int32)[:, None]
    ).astype(jnp.bfloat16)
    packed = (
        jnp.dot(table, normed, preferred_element_type=jnp.float32)
        .astype(jnp.bfloat16)
        .reshape(airborne_expert, capacity, D)
    )
    outgoing = jnp.repeat(packed, SPLIT, axis=0)
    received = lax.all_to_all(outgoing, "expert", split_axis=0, concat_axis=0, tiled=True)
    row_block = received.reshape(devices * capacity, D)
    gated = jnp.dot(row_block, gate_proj[0, 0], preferred_element_type=jnp.float32)
    lifted = jnp.dot(row_block, up_proj[0, 0], preferred_element_type=jnp.float32)
    activation = (jax.nn.silu(gated) * lifted).astype(jnp.bfloat16)
    partial_value = jnp.dot(
        activation, down_proj[0, 0], preferred_element_type=jnp.float32
    ).reshape(devices, capacity, D)
    returned = lax.all_to_all(
        partial_value.astype(jnp.bfloat16), "expert", split_axis=0, concat_axis=0, tiled=True
    ).astype(partial_value.dtype)
    summed = jnp.sum(returned.reshape(airborne_expert, SPLIT, capacity, D), axis=1).reshape(
        airborne_expert * capacity, D
    )
    routed = summed[code]
    result = (mixed + merge_results[:, None] * routed).astype(jnp.bfloat16)
    return shifted(result[None], "section", 1)


MESH = pl.DeviceIdType.MESH
PIECES = 4
LINE = 4


def tick_kernel(
    sizes,
    rows_ref,
    fill_ref,
    gain_ref,
    label_ref,
    query_hbm,
    hidden_hbm,
    out_proj_hbm,
    router_hbm,
    gate_hbm,
    up_hbm,
    down_hbm,
    out_ref,
    out_proj_ref,
    router_ref,
    gate_ref,
    up_ref,
    down_ref,
    hidden_ref,
    query_all,
    rows_all,
    keys_ref,
    values_ref,
    attended_ref,
    pair_send,
    pair_recv,
    part_ref,
    inward_send,
    outward_send,
    near_recv,
    far_recv,
    normed_ref,
    mixed_ref,
    combine_ref,
    expert_send,
    expert_recv,
    routed_ref,
    back_send,
    back_recv,
    home_recv,
    result_ref,
    weight_sem,
    query_send_sem,
    query_recv_sem,
    rows_send_sem,
    rows_recv_sem,
    share_send_sem,
    share_recv_sem,
    pair_sem,
    near_sem,
    far_sem,
    fall_sem,
    norm_sem,
    expert_sem,
    back_sem,
    home_send_sem,
    home_recv_sem,
    out_sem,
):
    devices, sections, tokens, cache_rows, heads, head_group, local_experts = sizes
    chips = devices // 2
    width = hidden_ref.shape[1] // PIECES
    section = lax.axis_index("section")
    me = lax.axis_index("expert")
    chip, core = me // 2, me % 2
    partner = me + 1 - 2 * core
    next_section = (section + 1) % sections
    before_section = (section + sections - 1) % sections
    toward = jnp.where(chip < 2, 2, -2)
    inward = me + toward
    outward = (me + devices - toward) % devices
    inner = (chip == 1) | (chip == 2)
    side = chip // 2
    features = query_all.shape[2]

    def remote(source, target, send_sem, recv_sem, to, to_section=None):
        return pltpu.make_async_remote_copy(
            src_ref=source,
            dst_ref=target,
            send_sem=send_sem,
            recv_sem=recv_sem,
            device_id=(section if to_section is None else to_section, to),
            device_id_type=MESH,
        )

    weights = [
        pltpu.make_async_copy(source, target, weight_sem.at[at])
        for at, (source, target) in enumerate(
            [
                (out_proj_hbm.at[0], out_proj_ref),
                (hidden_hbm.at[0], hidden_ref),
                (gate_hbm.at[0, 0], gate_ref),
                (up_hbm.at[0, 0], up_ref),
                (down_hbm.at[0, 0], down_ref),
                (router_hbm.at[0], router_ref),
            ]
        )
    ]

    barrier = pltpu.get_barrier_semaphore()
    for step in range(1, devices):
        pl.semaphore_signal(
            barrier, inc=1, device_id=(section, (me + step) % devices), device_id_type=MESH
        )
    pl.semaphore_signal(barrier, inc=1, device_id=(next_section, me), device_id_type=MESH)
    pl.semaphore_signal(barrier, inc=1, device_id=(before_section, me), device_id_type=MESH)
    pl.semaphore_wait(barrier, devices + 1)

    def key_head(chip_at):
        return (chip_at * 2 * heads) // head_group

    def query_part(to):
        return query_hbm.at[0, :, pl.ds(pl.multiple_of(to * features, HEAD_SIZE), features)]

    def query_copy(step):
        to = (me + step) % devices
        return remote(
            query_part(to),
            query_all.at[me],
            query_send_sem.at[step],
            query_recv_sem.at[step],
            to,
        )

    own_query = pltpu.make_async_copy(query_part(me), query_all.at[me], query_recv_sem.at[0])

    def rows_copy(step):
        to_chip = (chip + step) % chips
        return remote(
            rows_ref.at[key_head(to_chip)],
            rows_all.at[me],
            rows_send_sem.at[step],
            rows_recv_sem.at[step],
            2 * to_chip + core,
        )

    def share_copy(step):
        slot = 2 * ((chip + chips - step) % chips) + core
        return remote(
            rows_all.at[slot],
            rows_all.at[slot],
            share_send_sem.at[step],
            share_recv_sem.at[step],
            partner,
        )

    for step in range(1, chips):
        rows_copy(step).start()
    for step in range(1, devices):
        query_copy(step).start()
    for copy in weights:
        copy.start()
    own_query.start()
    rows_all[me] = rows_ref[key_head(chip)]
    for step in range(chips):
        if step > 0:
            rows_copy(step).wait_recv()
        share_copy(step).start()
    for step in range(chips):
        share_copy(step).wait_recv()

    for device in range(devices):
        at = 0
        for ref in (keys_ref, values_ref):
            start = devices * cache_rows + device * tokens
            ref[start : start + tokens] = rows_all[device, at : at + tokens]
            at += tokens
        for ref in (keys_ref, values_ref):
            start = device * cache_rows
            ref[start : start + cache_rows] = rows_all[device, at : at + cache_rows]
            at += cache_rows
    own_query.wait()
    for step in range(1, devices):
        query_copy(step).wait_recv()
    for copy in weights[:2]:
        copy.wait()

    fill = fill_ref[0]
    total_rows = keys_ref.shape[0]
    cached = devices * cache_rows
    group_rows = heads * tokens
    column = lax.broadcasted_iota(jnp.int32, (group_rows, total_rows), 1)
    row_token = lax.broadcasted_iota(jnp.int32, (group_rows, total_rows), 0) % tokens

    def home_of(step):
        return jnp.where(step % 2 == 0, step // 2, chips - 1 - step // 2)

    def piece_copy(source, target, sems, step, piece, to):
        return remote(
            source.at[step, piece],
            target.at[step, piece],
            sems.at[0, step, piece],
            sems.at[1, step, piece],
            to,
        )

    def pair_copy(step, piece):
        return piece_copy(pair_send, pair_recv, pair_sem, step, piece, partner)

    def near_copy(step, piece):
        return piece_copy(inward_send, near_recv, near_sem, step, piece, inward)

    def far_copy(step, piece):
        return piece_copy(inward_send, far_recv, far_sem, step, piece, inward)

    def fall_copy(step, piece):
        return remote(
            outward_send.at[step, piece],
            far_recv.at[step, piece],
            fall_sem.at[step, piece],
            far_sem.at[1, step, piece],
            outward,
        )

    def expert_copy(step, piece):
        return piece_copy(expert_send, expert_recv, expert_sem, step, piece, partner)

    def back_copy(step, piece):
        return piece_copy(back_send, back_recv, back_sem, step, piece, inward)

    def home_copy(step, piece, from_side):
        return remote(
            back_send.at[step, piece],
            home_recv.at[from_side, piece],
            home_send_sem.at[step, piece],
            home_recv_sem.at[from_side, piece],
            2 * home_of(step) + core,
        )

    def norm_copy(step):
        return remote(
            normed_ref.at[step, 0],
            normed_ref.at[step, 1],
            norm_sem.at[0, step],
            norm_sem.at[1, step],
            partner,
        )

    def out_copy(piece):
        return remote(
            result_ref.at[piece],
            out_ref.at[:, pl.ds(piece * width, width)],
            out_sem.at[0, piece],
            out_sem.at[1, piece],
            me,
            next_section,
        )

    def project(step):
        home = home_of(step)
        for which in range(2):
            owner = 2 * home + (core if which == 0 else 1 - core)
            scores = (
                lax.dot_general(
                    jnp.concatenate(
                        [
                            query_all[owner, :, head * HEAD_SIZE : (head + 1) * HEAD_SIZE]
                            for head in range(heads)
                        ],
                        axis=0,
                    ),
                    keys_ref[...],
                    (((1,), (1,)), ((), ())),
                    preferred_element_type=jnp.float32,
                )
                * (1.0 / math.sqrt(HEAD_SIZE))
            )
            limit = jnp.where(column < cached, fill, cached + owner * tokens + row_token + 1)
            visible = column < limit
            masked = jnp.where(visible, scores, -1e30)
            highest = jnp.max(masked, axis=1, keepdims=True)
            weight = jnp.where(visible, jnp.exp(masked - highest), 0.0)
            totals = jnp.sum(weight, axis=1, keepdims=True)
            mean = (
                jnp.dot(
                    weight.astype(jnp.bfloat16), values_ref[...], preferred_element_type=jnp.float32
                )
                / totals
            ).astype(jnp.bfloat16)
            for head in range(heads):
                attended_ref[
                    which * tokens : (which + 1) * tokens, head * HEAD_SIZE : (head + 1) * HEAD_SIZE
                ] = mean[head * tokens : (head + 1) * tokens]
        for piece in range(PIECES):
            product = jnp.dot(
                attended_ref[...],
                out_proj_ref[:, piece * width : (piece + 1) * width],
                preferred_element_type=jnp.float32,
            )
            part_ref[step, piece] = product[:tokens]
            pair_send[step, piece] = product[tokens:].astype(jnp.bfloat16)
            pair_copy(step, piece).start()

        @pl.when(home == chip)
        def _():
            for piece in range(PIECES):
                part_ref[step, piece] += hidden_ref[
                    :, piece * width : (piece + 1) * width
                ].astype(jnp.float32)

        for piece in range(PIECES):
            pair_copy(step, piece).wait_recv()
            part_ref[step, piece] += pair_recv[step, piece].astype(jnp.float32)

            @pl.when(jnp.logical_not(inner))
            def _():
                inward_send[step, piece] = part_ref[step, piece].astype(jnp.bfloat16)
                near_copy(step, piece).start()

    def forward(step):
        for piece in range(PIECES):
            near_copy(step, piece).wait_recv()
            inward_send[step, piece] = (
                part_ref[step, piece] + near_recv[step, piece].astype(jnp.float32)
            ).astype(jnp.bfloat16)
            far_copy(step, piece).start()

    my_expert = (me // SPLIT).astype(jnp.float32)
    select_at = 2 * tokens + 2 * cache_rows

    def layer(step):
        home = home_of(step)

        @pl.when(step == 0)
        def _():
            for copy in weights[2:]:
                copy.wait()

        for piece in range(PIECES):
            far_copy(step, piece).wait_recv()
            part_ref[step, piece] += far_recv[step, piece].astype(jnp.float32)

            @pl.when(inner)
            def _():
                outward_send[step, piece] = part_ref[step, piece].astype(jnp.bfloat16)
                fall_copy(step, piece).start()
                part_ref[step, piece] += near_recv[step, piece].astype(jnp.float32)

        squares = jnp.zeros((tokens, 1), jnp.float32)
        for piece in range(PIECES):
            mixed = part_ref[step, piece]
            squares += jnp.sum(mixed * mixed, axis=1, keepdims=True)
        inverse = lax.rsqrt(squares / (PIECES * width) + 1e-06)
        for piece in range(PIECES):
            columns = slice(piece * width, (piece + 1) * width)
            normed_ref[step, 0, :, columns] = (
                part_ref[step, piece] * inverse * gain_ref[:, columns].astype(jnp.float32)
            ).astype(jnp.bfloat16)
        norm_copy(step).start()

        @pl.when(home == chip)
        def _():
            for piece in range(PIECES):
                mixed_ref[piece] = part_ref[step, piece]
            logits = jnp.dot(
                normed_ref[step, 0], router_ref[...], preferred_element_type=jnp.float32
            )
            labels = label_ref[...]
            expert_at = lax.broadcasted_iota(jnp.int32, logits.shape, 1)
            picked = []
            for at in range(labels.shape[1]):
                match = labels[:, at : at + 1] == expert_at
                picked.append(jnp.sum(jnp.where(match, logits, 0.0), axis=1, keepdims=True))
            highest = picked[0]
            for value in picked[1:]:
                highest = jnp.maximum(highest, value)
            total = jnp.zeros_like(highest)
            chosen = jnp.zeros_like(highest)
            for at, value in enumerate(picked):
                weight = jnp.exp(value - highest)
                total += weight
                chosen += jnp.where(labels[:, at : at + 1] < local_experts, weight, 0.0)
            combine_ref[...] = jnp.broadcast_to(chosen / total, combine_ref.shape)

        norm_copy(step).wait_recv()
        rows = normed_ref[step].reshape(2 * tokens, PIECES * width)
        gated = jnp.dot(rows, gate_ref[...], preferred_element_type=jnp.float32)
        lifted = jnp.dot(rows, up_ref[...], preferred_element_type=jnp.float32)
        activation = gated / (1.0 + jnp.exp(-gated)) * lifted
        selected = jnp.concatenate(
            [
                rows_all[2 * home + core, select_at : select_at + tokens],
                rows_all[2 * home + 1 - core, select_at : select_at + tokens],
            ],
            axis=0,
        ).astype(jnp.float32)[:, :1]
        activation = jnp.where(selected == my_expert, activation, 0.0).astype(jnp.bfloat16)
        for piece in range(PIECES):
            product = jnp.dot(
                activation,
                down_ref[:, piece * width : (piece + 1) * width],
                preferred_element_type=jnp.float32,
            )
            routed_ref[step, piece] = product[:tokens]
            expert_send[step, piece] = product[tokens:].astype(jnp.bfloat16)
            expert_copy(step, piece).start()
        for piece in range(PIECES):
            expert_copy(step, piece).wait_recv()
            routed_ref[step, piece] += expert_recv[step, piece].astype(jnp.float32)

            @pl.when(jnp.logical_not(inner) & (home != chip))
            def _():
                back_send[step, piece] = routed_ref[step, piece].astype(jnp.bfloat16)
                back_copy(step, piece).start()

    def outer_chip():
        return 3 * side

    def fold(step):
        home = home_of(step)
        for piece in range(PIECES):

            @pl.when(home != outer_chip())
            def _():
                back_copy(step, piece).wait_recv()
                routed_ref[step, piece] += back_recv[step, piece].astype(jnp.float32)

            @pl.when(home != chip)
            def _():
                back_send[step, piece] = routed_ref[step, piece].astype(jnp.bfloat16)
                home_copy(step, piece, side).start()

    def finish(step):
        for piece in range(PIECES):
            for from_side in range(2):

                @pl.when(chip != from_side + 1)
                def _():
                    home_copy(step, piece, from_side).wait_recv()
                    routed_ref[step, piece] += home_recv[from_side, piece].astype(jnp.float32)

            result_ref[piece] = (
                mixed_ref[piece] + combine_ref[:, :1] * routed_ref[step, piece]
            ).astype(jnp.bfloat16)
            out_copy(piece).start()

    def within(step):
        return (step >= 0) & (step < chips)

    def turn(time, carry):
        pl.when(within(time))(lambda: project(time))
        pl.when(within(time - 1) & inner)(lambda: forward(time - 1))
        pl.when(within(time - 4) & inner)(lambda: fold(time - 4))
        layer_step = time - jnp.where(inner, 2, 3)
        pl.when(within(layer_step))(lambda: layer(layer_step))
        ending = time - 5
        pl.when(within(ending) & (home_of(ending) == chip))(lambda: finish(ending))
        return carry

    lax.fori_loop(0, chips + 5, turn, 0)

    def drain(step, carry):
        home = home_of(step)
        norm_copy(step).wait_send()
        for piece in range(PIECES):
            pair_copy(step, piece).wait_send()
            expert_copy(step, piece).wait_send()

            @pl.when(inner)
            def _():
                far_copy(step, piece).wait_send()
                fall_copy(step, piece).wait_send()

            @pl.when(jnp.logical_not(inner))
            def _():
                near_copy(step, piece).wait_send()

            @pl.when(inner & (home != chip))
            def _():
                home_copy(step, piece, side).wait_send()

            @pl.when(jnp.logical_not(inner) & (home != chip))
            def _():
                back_copy(step, piece).wait_send()

        return carry

    lax.fori_loop(0, chips, drain, 0)
    for step in range(1, chips):
        rows_copy(step).wait_send()
    for step in range(chips):
        share_copy(step).wait_send()
    for step in range(1, devices):
        query_copy(step).wait_send()
    for piece in range(PIECES):
        out_copy(piece).wait()


def fused_shards(
    sections,
    hidden,
    queries,
    fresh_kv,
    cache_kv,
    cache_fill,
    out_proj,
    norm_gain,
    router_weight,
    expert_labels,
    gate_proj,
    up_proj,
    down_proj,
):
    devices = lax.axis_size("expert")
    chips = devices // 2
    tokens, model = hidden.shape[1:]
    cache_rows = cache_kv.shape[2]
    heads = QUERY_HEADS // devices
    head_group = QUERY_HEADS // KEY_VALUE_HEADS
    local_experts = devices // SPLIT
    features = heads * HEAD_SIZE
    hidden_units = gate_proj.shape[3]
    width = model // PIECES
    labels = expert_labels[0]
    selected = jnp.sum(jnp.where(labels < local_experts, labels, 0), axis=1)

    def by_head(array, length):
        return jnp.transpose(
            array.reshape(2, length, KEY_VALUE_HEADS, HEAD_SIZE), (2, 0, 1, 3)
        ).reshape(KEY_VALUE_HEADS, 2 * length, HEAD_SIZE)

    key_rows = jnp.concatenate(
        [
            by_head(fresh_kv[0], tokens),
            by_head(cache_kv[0], cache_rows),
            jnp.broadcast_to(
                selected.astype(jnp.bfloat16)[None, :, None], (KEY_VALUE_HEADS, tokens, HEAD_SIZE)
            ),
        ],
        axis=1,
    )
    message = key_rows.shape[1]
    bf16, f32 = jnp.bfloat16, jnp.float32
    vmem = pl.BlockSpec(memory_space=pltpu.VMEM)
    anywhere = pl.BlockSpec(memory_space=pl.ANY)
    block = (chips, PIECES, tokens, width)
    dma = pltpu.SemaphoreType.DMA
    sizes = (devices, sections, tokens, cache_rows, heads, head_group, local_experts)
    total_rows = devices * (tokens + cache_rows)
    result = pl.pallas_call(
        functools.partial(tick_kernel, sizes),
        out_shape=jax.ShapeDtypeStruct((tokens, model), bf16),
        in_specs=[vmem, pl.BlockSpec(memory_space=pltpu.SMEM), vmem, vmem] + [anywhere] * 7,
        out_specs=vmem,
        scratch_shapes=[
            pltpu.VMEM((features, model), bf16),
            pltpu.VMEM(router_weight.shape[1:], bf16),
            pltpu.VMEM((model, hidden_units), bf16),
            pltpu.VMEM((model, hidden_units), bf16),
            pltpu.VMEM((hidden_units, model), bf16),
            pltpu.VMEM((tokens, model), bf16),
            pltpu.VMEM((devices, tokens, features), bf16),
            pltpu.VMEM((devices, message, HEAD_SIZE), bf16),
            pltpu.VMEM((total_rows, HEAD_SIZE), bf16),
            pltpu.VMEM((total_rows, HEAD_SIZE), bf16),
            pltpu.VMEM((2 * tokens, features), bf16),
            pltpu.VMEM(block, bf16),
            pltpu.VMEM(block, bf16),
            pltpu.VMEM(block, f32),
            pltpu.VMEM(block, bf16),
            pltpu.VMEM(block, bf16),
            pltpu.VMEM(block, bf16),
            pltpu.VMEM(block, bf16),
            pltpu.VMEM((chips, 2, tokens, model), bf16),
            pltpu.VMEM((PIECES, tokens, width), f32),
            pltpu.VMEM((tokens, 128), f32),
            pltpu.VMEM(block, bf16),
            pltpu.VMEM(block, bf16),
            pltpu.VMEM(block, f32),
            pltpu.VMEM(block, bf16),
            pltpu.VMEM(block, bf16),
            pltpu.VMEM((2, PIECES, tokens, width), bf16),
            pltpu.VMEM((PIECES, tokens, width), bf16),
            dma((6,)),
            dma((devices,)),
            dma((devices,)),
            dma((chips,)),
            dma((chips,)),
            dma((chips,)),
            dma((chips,)),
            dma((2, chips, PIECES)),
            dma((2, chips, PIECES)),
            dma((2, chips, PIECES)),
            dma((chips, PIECES)),
            dma((2, chips)),
            dma((2, chips, PIECES)),
            dma((2, chips, PIECES)),
            dma((chips, PIECES)),
            dma((2, PIECES)),
            dma((2, PIECES)),
        ],
        compiler_params=pltpu.CompilerParams(
            collective_id=0, has_side_effects=True, vmem_limit_bytes=60 * 2**20
        ),
    )(
        key_rows,
        cache_fill,
        norm_gain,
        labels,
        queries,
        hidden,
        out_proj,
        router_weight,
        gate_proj,
        up_proj,
        down_proj,
    )
    return result[None]


def fits_one_kernel(mesh):
    devices = mesh.shape["expert"]
    if devices != 2 * LINE or QUERY_HEADS % devices:
        return False
    return (QUERY_HEADS // KEY_VALUE_HEADS) % (2 * (QUERY_HEADS // devices)) == 0


def solution(mesh):
    in_specs = (
        P("section", "expert", None),
        P("section", "expert", None),
        P("section", None, "expert", None),
        P("section", None, "expert", None),
        P("section"),
        P("section", "expert", None),
        P("section", None),
        P("section", None, None),
        P("section", "expert", None),
        P("section", "expert", None, None),
        P("section", "expert", None, None),
        P("section", "expert", None, None),
    )
    out_specs = P("section", "expert", None)
    body = shards
    if fits_one_kernel(mesh):
        body = functools.partial(fused_shards, mesh.shape["section"])
    return jax.shard_map(body, mesh=mesh, in_specs=in_specs, out_specs=out_specs, check_vma=False)
```

```python
import functools
import math

import jax
import jax.numpy as jnp
from jax import lax
from jax.experimental import pallas as pl
from jax.experimental.pallas import tpu as pltpu
from jax.sharding import PartitionSpec as P

D = 4096
QUERY_HEADS = 32
KEY_VALUE_HEADS = 2
HEAD_SIZE = 128
EXPERTS = 128
SPLIT = 4


def shifted(shard, axis, by):
    length = lax.axis_size(axis)
    return lax.ppermute(shard, axis, [(i, (i + by) % length) for i in range(length)])


def shards(
    hidden,
    queries,
    fresh_kv,
    cache_kv,
    cache_fill,
    out_proj,
    norm_gain,
    router_weight,
    expert_labels,
    gate_proj,
    up_proj,
    down_proj,
):
    devices = lax.axis_size("expert")
    device_index = lax.axis_index("expert")
    section_tokens = hidden.shape[1]
    local_cache = cache_kv.shape[2]
    stride = local_cache + section_tokens
    head_group = QUERY_HEADS // KEY_VALUE_HEADS
    scale = 1.0 / math.sqrt(HEAD_SIZE)
    fill = cache_fill[0]
    query_pos = device_index * section_tokens + jnp.arange(section_tokens, dtype=jnp.int32)
    gathered_queries = queries[0].reshape(section_tokens, KEY_VALUE_HEADS, head_group, HEAD_SIZE)
    joined_rows = jnp.concatenate([cache_kv[0], fresh_kv[0]], axis=1)

    def attend_block(carry, block_key_value, start):
        run_max, run_sum, run_acc = carry
        token_count = block_key_value.shape[1]
        row_index = start + jnp.arange(token_count, dtype=jnp.int32)
        owner = row_index // stride
        offset = row_index % stride
        cache_pos = owner * local_cache + offset
        slice_pos = owner * section_tokens + offset - local_cache
        visible = jnp.where(
            offset[None, :] < local_cache,
            cache_pos[None, :] < fill,
            slice_pos[None, :] <= query_pos[:, None],
        )
        key_matrix = block_key_value[0].reshape(token_count, KEY_VALUE_HEADS, HEAD_SIZE)
        value_matrix = block_key_value[1].reshape(token_count, KEY_VALUE_HEADS, HEAD_SIZE)
        scores = (
            jnp.einsum(
                "tgkd,rgd->tgkr", gathered_queries, key_matrix, preferred_element_type=jnp.float32
            )
            * scale
        )
        mask = visible[:, None, None, :]
        masked = jnp.where(mask, scores, -1e30)
        new_max = jnp.maximum(run_max, jnp.max(masked, axis=3))
        weights = jnp.where(mask, jnp.exp(masked - new_max[..., None]), 0.0)
        factor = jnp.exp(run_max - new_max)
        new_sum = run_sum * factor + jnp.sum(weights, axis=3)
        rounded = weights.astype(jnp.bfloat16)
        new_acc = run_acc * factor[..., None] + jnp.einsum(
            "tgkr,rgd->tgkd", rounded, value_matrix, preferred_element_type=jnp.float32
        )
        return (new_max, new_sum, new_acc)

    def attend_piece(carry, piece, start):
        token_count = piece.shape[1]
        cache_block = token_count
        while cache_block > 1024 and cache_block % 2 == 0:
            cache_block = cache_block // 2
        relay_steps = token_count // cache_block
        if relay_steps == 1:
            return attend_block(carry, piece, start)
        cache_blocks = jnp.transpose(
            piece.reshape(2, relay_steps, cache_block, KEY_VALUE_HEADS * HEAD_SIZE), (1, 0, 2, 3)
        )
        offsets = start + jnp.arange(relay_steps, dtype=jnp.int32) * cache_block

        def one_step(state, item):
            block_key_value, first = item
            return (attend_block(state, block_key_value, first), None)

        final, unused = lax.scan(one_step, carry, (cache_blocks, offsets))
        return final

    initial_maximum = jnp.full((section_tokens, KEY_VALUE_HEADS, head_group), -1e30, jnp.float32)
    initial_sum = jnp.zeros((section_tokens, KEY_VALUE_HEADS, head_group), jnp.float32)
    initial_accumulator = jnp.zeros(
        (section_tokens, KEY_VALUE_HEADS, head_group, HEAD_SIZE), jnp.float32
    )
    every_key_value = lax.all_gather(joined_rows, "expert", axis=1, tiled=True)
    final_max, final_sum, final_acc = attend_piece(
        (initial_maximum, initial_sum, initial_accumulator), every_key_value, jnp.int32(0)
    )
    attended = (
        (final_acc / final_sum[..., None])
        .reshape(section_tokens, QUERY_HEADS * HEAD_SIZE)
        .astype(jnp.bfloat16)
    )
    features = lax.all_to_all(attended, "expert", split_axis=1, concat_axis=0, tiled=True)
    partial_projected = jnp.dot(features, out_proj[0], preferred_element_type=jnp.float32)
    projected = lax.psum_scatter(
        partial_projected.astype(jnp.bfloat16), "expert", scatter_dimension=0, tiled=True
    ).astype(jnp.float32)
    mixed = hidden[0].astype(jnp.float32) + projected
    inverse = lax.rsqrt(jnp.mean(mixed * mixed, axis=1, keepdims=True) + 1e-06)
    normed = (mixed * inverse * norm_gain[0].astype(jnp.float32)[None, :]).astype(jnp.bfloat16)
    logits = jnp.dot(normed, router_weight[0], preferred_element_type=jnp.float32)
    label_rows = expert_labels[0]
    matches = label_rows[:, :, None] == jnp.arange(EXPERTS, dtype=jnp.int32)[None, None, :]
    picked = jnp.sum(jnp.where(matches, logits[:, None, :], 0.0), axis=2)
    probabilities = jax.nn.softmax(picked, axis=1)
    airborne_expert = devices // SPLIT
    hot_rows = SPLIT * max(1, section_tokens // (8 * SPLIT))
    other_rows = (section_tokens - hot_rows + airborne_expert - 2) // (airborne_expert - 1)
    capacity = SPLIT * ((max(hot_rows, other_rows) + SPLIT - 1) // SPLIT)
    airborne_mask = label_rows < airborne_expert
    selected_experts = jnp.sum(jnp.where(airborne_mask, label_rows, 0), axis=1)
    merge_results = jnp.sum(jnp.where(airborne_mask, probabilities, 0.0), axis=1)
    member = (
        selected_experts[:, None] == jnp.arange(airborne_expert, dtype=jnp.int32)[None, :]
    ).astype(jnp.int32)
    earlier = jnp.cumsum(member, axis=0) - member
    slot = jnp.sum(earlier * member, axis=1)
    code = selected_experts * capacity + slot
    table = (
        code[None, :] == jnp.arange(airborne_expert * capacity, dtype=jnp.int32)[:, None]
    ).astype(jnp.bfloat16)
    packed = (
        jnp.dot(table, normed, preferred_element_type=jnp.float32)
        .astype(jnp.bfloat16)
        .reshape(airborne_expert, capacity, D)
    )
    outgoing = jnp.repeat(packed, SPLIT, axis=0)
    received = lax.all_to_all(outgoing, "expert", split_axis=0, concat_axis=0, tiled=True)
    row_block = received.reshape(devices * capacity, D)
    gated = jnp.dot(row_block, gate_proj[0, 0], preferred_element_type=jnp.float32)
    lifted = jnp.dot(row_block, up_proj[0, 0], preferred_element_type=jnp.float32)
    activation = (jax.nn.silu(gated) * lifted).astype(jnp.bfloat16)
    partial_value = jnp.dot(
        activation, down_proj[0, 0], preferred_element_type=jnp.float32
    ).reshape(devices, capacity, D)
    returned = lax.all_to_all(
        partial_value.astype(jnp.bfloat16), "expert", split_axis=0, concat_axis=0, tiled=True
    ).astype(partial_value.dtype)
    summed = jnp.sum(returned.reshape(airborne_expert, SPLIT, capacity, D), axis=1).reshape(
        airborne_expert * capacity, D
    )
    routed = summed[code]
    result = (mixed + merge_results[:, None] * routed).astype(jnp.bfloat16)
    return shifted(result[None], "section", 1)


MESH = pl.DeviceIdType.MESH
PIECES = 4
LINE = 4


def tick_kernel(
    sizes,
    rows_ref,
    fill_ref,
    gain_ref,
    label_ref,
    query_hbm,
    hidden_hbm,
    out_proj_hbm,
    router_hbm,
    gate_hbm,
    up_hbm,
    down_hbm,
    out_ref,
    out_proj_ref,
    router_ref,
    widen_ref,
    down_ref,
    hidden_ref,
    query_all,
    rows_all,
    keys_ref,
    values_ref,
    relation_ref,
    attended_ref,
    pair_send,
    pair_recv,
    part_ref,
    inward_send,
    outward_send,
    near_recv,
    far_recv,
    normed_ref,
    mixed_ref,
    combine_ref,
    expert_send,
    expert_recv,
    routed_ref,
    back_send,
    back_recv,
    home_recv,
    result_ref,
    weight_sem,
    query_send_sem,
    query_recv_sem,
    rows_send_sem,
    rows_recv_sem,
    share_send_sem,
    share_recv_sem,
    pair_sem,
    near_sem,
    far_sem,
    fall_sem,
    norm_sem,
    expert_sem,
    back_sem,
    home_send_sem,
    home_recv_sem,
    out_sem,
):
    devices, sections, tokens, cache_rows, heads, head_group, local_experts = sizes
    chips = devices // 2
    width = hidden_ref.shape[1] // PIECES
    section = lax.axis_index("section")
    me = lax.axis_index("expert")
    chip, core = me // 2, me % 2
    partner = me + 1 - 2 * core
    next_section = (section + 1) % sections
    before_section = (section + sections - 1) % sections
    toward = jnp.where(chip < 2, 2, -2)
    inward = me + toward
    outward = (me + devices - toward) % devices
    inner = (chip == 1) | (chip == 2)
    side = chip // 2
    features = query_all.shape[2]
    units = down_ref.shape[0]

    def remote(source, target, send_sem, recv_sem, to, to_section=None):
        return pltpu.make_async_remote_copy(
            src_ref=source,
            dst_ref=target,
            send_sem=send_sem,
            recv_sem=recv_sem,
            device_id=(section if to_section is None else to_section, to),
            device_id_type=MESH,
        )

    weights = [
        pltpu.make_async_copy(source, target, weight_sem.at[at])
        for at, (source, target) in enumerate(
            [
                (out_proj_hbm.at[0], out_proj_ref),
                (hidden_hbm.at[0], hidden_ref),
                (gate_hbm.at[0, 0], widen_ref.at[:, :units]),
                (up_hbm.at[0, 0], widen_ref.at[:, units:]),
                (down_hbm.at[0, 0], down_ref),
                (router_hbm.at[0], router_ref),
            ]
        )
    ]

    barrier = pltpu.get_barrier_semaphore()
    for step in range(1, devices):
        pl.semaphore_signal(
            barrier, inc=1, device_id=(section, (me + step) % devices), device_id_type=MESH
        )
    pl.semaphore_signal(barrier, inc=1, device_id=(next_section, me), device_id_type=MESH)
    pl.semaphore_signal(barrier, inc=1, device_id=(before_section, me), device_id_type=MESH)
    pl.semaphore_wait(barrier, devices + 1)

    def key_head(chip_at):
        return (chip_at * 2 * heads) // head_group

    def query_part(to):
        return query_hbm.at[0, :, pl.ds(pl.multiple_of(to * features, HEAD_SIZE), features)]

    def query_copy(step):
        to = (me + step) % devices
        return remote(
            query_part(to),
            query_all.at[me],
            query_send_sem.at[step],
            query_recv_sem.at[step],
            to,
        )

    own_query = pltpu.make_async_copy(query_part(me), query_all.at[me], query_recv_sem.at[0])

    def rows_copy(step):
        to_chip = (chip + step) % chips
        return remote(
            rows_ref.at[key_head(to_chip)],
            rows_all.at[me],
            rows_send_sem.at[step],
            rows_recv_sem.at[step],
            2 * to_chip + core,
        )

    def share_copy(step):
        slot = 2 * ((chip + chips - step) % chips) + core
        return remote(
            rows_all.at[slot],
            rows_all.at[slot],
            share_send_sem.at[step],
            share_recv_sem.at[step],
            partner,
        )

    for step in range(1, chips):
        rows_copy(step).start()
    def send_queries():
        for step in range(1, devices):
            query_copy(step).start()

    pl.when(jnp.logical_not(inner))(send_queries)
    for copy in weights:
        copy.start()
    own_query.start()
    rows_all[me] = rows_ref[key_head(chip)]
    for step in range(chips):
        if step > 0:
            rows_copy(step).wait_recv()
        share_copy(step).start()
    for step in range(chips):
        share_copy(step).wait_recv()

    for device in range(devices):
        at = 0
        for ref in (keys_ref, values_ref):
            start = devices * cache_rows + device * tokens
            ref[start : start + tokens, :HEAD_SIZE] = rows_all[device, at : at + tokens]
            at += tokens
        for ref in (keys_ref, values_ref):
            start = device * cache_rows
            ref[start : start + cache_rows, :HEAD_SIZE] = rows_all[device, at : at + cache_rows]
            at += cache_rows
    own_query.wait()
    for copy in weights[:2]:
        copy.wait()

    fill = fill_ref[0]
    total_rows = keys_ref.shape[0]
    cached = devices * cache_rows
    group_rows = heads * tokens
    column = lax.broadcasted_iota(jnp.int32, (group_rows, total_rows), 1)
    row_token = lax.broadcasted_iota(jnp.int32, (group_rows, total_rows), 0) % tokens
    relation_ref[...] = jnp.where(column < cached, column, column - cached - row_token)
    values_ref[:, HEAD_SIZE:] = jnp.ones((total_rows, HEAD_SIZE), jnp.bfloat16)
    first_row = lax.broadcasted_iota(jnp.int32, (1, total_rows), 1)

    def home_of(step):
        return jnp.where(step % 2 == 0, step // 2, chips - 1 - step // 2)

    def piece_copy(source, target, sems, step, piece, to):
        return remote(
            source.at[step, piece],
            target.at[step, piece],
            sems.at[0, step, piece],
            sems.at[1, step, piece],
            to,
        )

    def pair_copy(step, piece):
        return piece_copy(pair_send, pair_recv, pair_sem, step, piece, partner)

    def near_copy(step, piece):
        return piece_copy(inward_send, near_recv, near_sem, step, piece, inward)

    def far_copy(step, piece):
        return piece_copy(inward_send, far_recv, far_sem, step, piece, inward)

    def fall_copy(step, piece):
        return remote(
            outward_send.at[step, piece],
            far_recv.at[step, piece],
            fall_sem.at[step, piece],
            far_sem.at[1, step, piece],
            outward,
        )

    def expert_copy(step, piece):
        return piece_copy(expert_send, expert_recv, expert_sem, step, piece, partner)

    def back_copy(step, piece):
        return piece_copy(back_send, back_recv, back_sem, step, piece, inward)

    def home_copy(step, piece, from_side):
        return remote(
            back_send.at[step, piece],
            home_recv.at[from_side, piece],
            home_send_sem.at[step, piece],
            home_recv_sem.at[from_side, piece],
            2 * home_of(step) + core,
        )

    def norm_copy(step, piece):
        return remote(
            normed_ref.at[step, piece, pl.ds(0, tokens)],
            normed_ref.at[step, piece, pl.ds(tokens, tokens)],
            norm_sem.at[0, step, piece],
            norm_sem.at[1, step, piece],
            partner,
        )

    def out_copy(piece):
        return remote(
            result_ref.at[piece],
            out_ref.at[:, pl.ds(piece * width, width)],
            out_sem.at[0, piece],
            out_sem.at[1, piece],
            me,
            next_section,
        )

    def project(step):
        home = home_of(step)
        for which in range(2):
            owner = 2 * home + (core if which == 0 else 1 - core)
            @pl.when(owner != me)
            def _():
                query_copy((me + devices - owner) % devices).wait_recv()

            scores = lax.dot_general(
                jnp.concatenate(
                    [
                        query_all[owner, :, head * HEAD_SIZE : (head + 1) * HEAD_SIZE]
                        for head in range(heads)
                    ],
                    axis=0,
                ),
                keys_ref[...],
                (((1,), (1,)), ((), ())),
                preferred_element_type=jnp.float32,
            )
            limit = jnp.where(first_row < cached, fill, owner * tokens + 1)
            masked = jnp.where(relation_ref[...] < limit, scores, -1e30)
            highest = jnp.max(masked, axis=1, keepdims=True)
            weight = jnp.exp2(
                (masked - highest) * (1.0 / (math.sqrt(HEAD_SIZE) * math.log(2.0)))
            )
            summed = jnp.dot(
                weight.astype(jnp.bfloat16), values_ref[...], preferred_element_type=jnp.float32
            )
            mean = (summed[:, :HEAD_SIZE] / summed[:, HEAD_SIZE:]).astype(jnp.bfloat16)
            for head in range(heads):
                attended_ref[
                    which * tokens : (which + 1) * tokens, head * HEAD_SIZE : (head + 1) * HEAD_SIZE
                ] = mean[head * tokens : (head + 1) * tokens]
        for piece in range(PIECES):
            product = jnp.dot(
                attended_ref[...],
                out_proj_ref[:, piece * width : (piece + 1) * width],
                preferred_element_type=jnp.float32,
            )
            part_ref[step, piece] = product[:tokens]
            pair_send[step, piece] = product[tokens:].astype(jnp.bfloat16)
            pair_copy(step, piece).start()

        @pl.when(home == chip)
        def _():
            for piece in range(PIECES):
                part_ref[step, piece] += hidden_ref[
                    :, piece * width : (piece + 1) * width
                ].astype(jnp.float32)

        for piece in range(PIECES):
            pair_copy(step, piece).wait_recv()
            part_ref[step, piece] += pair_recv[step, piece].astype(jnp.float32)

            @pl.when(jnp.logical_not(inner))
            def _():
                inward_send[step, piece] = part_ref[step, piece].astype(jnp.bfloat16)
                near_copy(step, piece).start()

    def forward(step):
        for piece in range(PIECES):
            near_copy(step, piece).wait_recv()
            inward_send[step, piece] = (
                part_ref[step, piece] + near_recv[step, piece].astype(jnp.float32)
            ).astype(jnp.bfloat16)
            far_copy(step, piece).start()

    my_expert = (me // SPLIT).astype(jnp.float32)
    select_at = 2 * tokens + 2 * cache_rows

    def layer(step):
        home = home_of(step)

        @pl.when(step == 0)
        def _():
            for copy in weights[2:]:
                copy.wait()

        for piece in range(PIECES):
            far_copy(step, piece).wait_recv()
            part_ref[step, piece] += far_recv[step, piece].astype(jnp.float32)

            @pl.when(inner)
            def _():
                outward_send[step, piece] = part_ref[step, piece].astype(jnp.bfloat16)
                fall_copy(step, piece).start()
                part_ref[step, piece] += near_recv[step, piece].astype(jnp.float32)

        squares = jnp.zeros((tokens, 1), jnp.float32)
        for piece in range(PIECES):
            mixed = part_ref[step, piece]
            squares += jnp.sum(mixed * mixed, axis=1, keepdims=True)
        inverse = lax.rsqrt(squares / (PIECES * width) + 1e-06)
        for piece in range(PIECES):
            columns = slice(piece * width, (piece + 1) * width)
            normed_ref[step, piece, :tokens] = (
                part_ref[step, piece] * inverse * gain_ref[:, columns].astype(jnp.float32)
            ).astype(jnp.bfloat16)
            norm_copy(step, piece).start()

        @pl.when(home == chip)
        def _():
            for piece in range(PIECES):
                mixed_ref[piece] = part_ref[step, piece]
            logits = jnp.zeros((tokens, router_ref.shape[1]), jnp.float32)
            for piece in range(PIECES):
                logits += jnp.dot(
                    normed_ref[step, piece, :tokens],
                    router_ref[piece * width : (piece + 1) * width],
                    preferred_element_type=jnp.float32,
                )
            labels = label_ref[...]
            expert_at = lax.broadcasted_iota(jnp.int32, logits.shape, 1)
            picked = []
            for at in range(labels.shape[1]):
                match = labels[:, at : at + 1] == expert_at
                picked.append(jnp.sum(jnp.where(match, logits, 0.0), axis=1, keepdims=True))
            highest = picked[0]
            for value in picked[1:]:
                highest = jnp.maximum(highest, value)
            total = jnp.zeros_like(highest)
            chosen = jnp.zeros_like(highest)
            for at, value in enumerate(picked):
                weight = jnp.exp(value - highest)
                total += weight
                chosen += jnp.where(labels[:, at : at + 1] < local_experts, weight, 0.0)
            combine_ref[...] = jnp.broadcast_to(chosen / total, combine_ref.shape)

        widened = jnp.zeros((2 * tokens, 2 * units), jnp.float32)
        for piece in range(PIECES):
            norm_copy(step, piece).wait_recv()
            widened += jnp.dot(
                normed_ref[step, piece],
                widen_ref[piece * width : (piece + 1) * width],
                preferred_element_type=jnp.float32,
            )
        gated, lifted = widened[:, :units], widened[:, units:]
        activation = gated / (1.0 + jnp.exp(-gated)) * lifted
        selected = jnp.concatenate(
            [
                rows_all[2 * home + core, select_at : select_at + tokens],
                rows_all[2 * home + 1 - core, select_at : select_at + tokens],
            ],
            axis=0,
        ).astype(jnp.float32)[:, :1]
        activation = jnp.where(selected == my_expert, activation, 0.0).astype(jnp.bfloat16)
        for piece in range(PIECES):
            product = jnp.dot(
                activation,
                down_ref[:, piece * width : (piece + 1) * width],
                preferred_element_type=jnp.float32,
            )
            routed_ref[step, piece] = product[:tokens]
            expert_send[step, piece] = product[tokens:].astype(jnp.bfloat16)
            expert_copy(step, piece).start()
        for piece in range(PIECES):
            expert_copy(step, piece).wait_recv()
            routed_ref[step, piece] += expert_recv[step, piece].astype(jnp.float32)

            @pl.when(jnp.logical_not(inner) & (home != chip))
            def _():
                back_send[step, piece] = routed_ref[step, piece].astype(jnp.bfloat16)
                back_copy(step, piece).start()

    def outer_chip():
        return 3 * side

    def fold(step):
        home = home_of(step)
        for piece in range(PIECES):

            @pl.when(home != outer_chip())
            def _():
                back_copy(step, piece).wait_recv()
                routed_ref[step, piece] += back_recv[step, piece].astype(jnp.float32)

            @pl.when(home != chip)
            def _():
                back_send[step, piece] = routed_ref[step, piece].astype(jnp.bfloat16)
                home_copy(step, piece, side).start()

    def finish(step):
        for piece in range(PIECES):
            for from_side in range(2):

                @pl.when(chip != from_side + 1)
                def _():
                    home_copy(step, piece, from_side).wait_recv()
                    routed_ref[step, piece] += home_recv[from_side, piece].astype(jnp.float32)

            result_ref[piece] = (
                mixed_ref[piece] + combine_ref[:, :1] * routed_ref[step, piece]
            ).astype(jnp.bfloat16)
            out_copy(piece).start()

    def within(step):
        return (step >= 0) & (step < chips)

    def turn(time, carry):
        pl.when(within(time))(lambda: project(time))
        pl.when((time == 0) & inner)(send_queries)
        pl.when(within(time - 1) & inner)(lambda: forward(time - 1))
        pl.when(within(time - 4) & inner)(lambda: fold(time - 4))
        layer_step = time - jnp.where(inner, 2, 3)
        pl.when(within(layer_step))(lambda: layer(layer_step))
        ending = time - 5
        pl.when(within(ending) & (home_of(ending) == chip))(lambda: finish(ending))
        return carry

    lax.fori_loop(0, chips + 5, turn, 0)

    def drain(step, carry):
        home = home_of(step)
        for piece in range(PIECES):
            norm_copy(step, piece).wait_send()
            pair_copy(step, piece).wait_send()
            expert_copy(step, piece).wait_send()

            @pl.when(inner)
            def _():
                far_copy(step, piece).wait_send()
                fall_copy(step, piece).wait_send()

            @pl.when(jnp.logical_not(inner))
            def _():
                near_copy(step, piece).wait_send()

            @pl.when(inner & (home != chip))
            def _():
                home_copy(step, piece, side).wait_send()

            @pl.when(jnp.logical_not(inner) & (home != chip))
            def _():
                back_copy(step, piece).wait_send()

        return carry

    lax.fori_loop(0, chips, drain, 0)
    for step in range(1, chips):
        rows_copy(step).wait_send()
    for step in range(chips):
        share_copy(step).wait_send()
    for step in range(1, devices):
        query_copy(step).wait_send()
    for piece in range(PIECES):
        out_copy(piece).wait()


def fused_shards(
    sections,
    hidden,
    queries,
    fresh_kv,
    cache_kv,
    cache_fill,
    out_proj,
    norm_gain,
    router_weight,
    expert_labels,
    gate_proj,
    up_proj,
    down_proj,
):
    devices = lax.axis_size("expert")
    chips = devices // 2
    tokens, model = hidden.shape[1:]
    cache_rows = cache_kv.shape[2]
    heads = QUERY_HEADS // devices
    head_group = QUERY_HEADS // KEY_VALUE_HEADS
    local_experts = devices // SPLIT
    features = heads * HEAD_SIZE
    hidden_units = gate_proj.shape[3]
    width = model // PIECES
    labels = expert_labels[0]
    selected = jnp.sum(jnp.where(labels < local_experts, labels, 0), axis=1)

    def by_head(array, length):
        return jnp.transpose(
            array.reshape(2, length, KEY_VALUE_HEADS, HEAD_SIZE), (2, 0, 1, 3)
        ).reshape(KEY_VALUE_HEADS, 2 * length, HEAD_SIZE)

    key_rows = jnp.concatenate(
        [
            by_head(fresh_kv[0], tokens),
            by_head(cache_kv[0], cache_rows),
            jnp.broadcast_to(
                selected.astype(jnp.bfloat16)[None, :, None], (KEY_VALUE_HEADS, tokens, HEAD_SIZE)
            ),
        ],
        axis=1,
    )
    message = key_rows.shape[1]
    bf16, f32 = jnp.bfloat16, jnp.float32
    vmem = pl.BlockSpec(memory_space=pltpu.VMEM)
    anywhere = pl.BlockSpec(memory_space=pl.ANY)
    block = (chips, PIECES, tokens, width)
    dma = pltpu.SemaphoreType.DMA
    sizes = (devices, sections, tokens, cache_rows, heads, head_group, local_experts)
    total_rows = devices * (tokens + cache_rows)
    result = pl.pallas_call(
        functools.partial(tick_kernel, sizes),
        out_shape=jax.ShapeDtypeStruct((tokens, model), bf16),
        in_specs=[vmem, pl.BlockSpec(memory_space=pltpu.SMEM), vmem, vmem] + [anywhere] * 7,
        out_specs=vmem,
        scratch_shapes=[
            pltpu.VMEM((features, model), bf16),
            pltpu.VMEM(router_weight.shape[1:], bf16),
            pltpu.VMEM((model, 2 * hidden_units), bf16),
            pltpu.VMEM((hidden_units, model), bf16),
            pltpu.VMEM((tokens, model), bf16),
            pltpu.VMEM((devices, tokens, features), bf16),
            pltpu.VMEM((devices, message, HEAD_SIZE), bf16),
            pltpu.VMEM((total_rows, HEAD_SIZE), bf16),
            pltpu.VMEM((total_rows, 2 * HEAD_SIZE), bf16),
            pltpu.VMEM((heads * tokens, total_rows), jnp.int32),
            pltpu.VMEM((2 * tokens, features), bf16),
            pltpu.VMEM(block, bf16),
            pltpu.VMEM(block, bf16),
            pltpu.VMEM(block, f32),
            pltpu.VMEM(block, bf16),
            pltpu.VMEM(block, bf16),
            pltpu.VMEM(block, bf16),
            pltpu.VMEM(block, bf16),
            pltpu.VMEM((chips, PIECES, 2 * tokens, width), bf16),
            pltpu.VMEM((PIECES, tokens, width), f32),
            pltpu.VMEM((tokens, 128), f32),
            pltpu.VMEM(block, bf16),
            pltpu.VMEM(block, bf16),
            pltpu.VMEM(block, f32),
            pltpu.VMEM(block, bf16),
            pltpu.VMEM(block, bf16),
            pltpu.VMEM((2, PIECES, tokens, width), bf16),
            pltpu.VMEM((PIECES, tokens, width), bf16),
            dma((6,)),
            dma((devices,)),
            dma((devices,)),
            dma((chips,)),
            dma((chips,)),
            dma((chips,)),
            dma((chips,)),
            dma((2, chips, PIECES)),
            dma((2, chips, PIECES)),
            dma((2, chips, PIECES)),
            dma((chips, PIECES)),
            dma((2, chips, PIECES)),
            dma((2, chips, PIECES)),
            dma((2, chips, PIECES)),
            dma((chips, PIECES)),
            dma((2, PIECES)),
            dma((2, PIECES)),
        ],
        compiler_params=pltpu.CompilerParams(
            collective_id=0, has_side_effects=True, vmem_limit_bytes=60 * 2**20
        ),
    )(
        key_rows,
        cache_fill,
        norm_gain,
        labels,
        queries,
        hidden,
        out_proj,
        router_weight,
        gate_proj,
        up_proj,
        down_proj,
    )
    return result[None]


def fits_one_kernel(mesh):
    devices = mesh.shape["expert"]
    if devices != 2 * LINE or QUERY_HEADS % devices:
        return False
    return (QUERY_HEADS // KEY_VALUE_HEADS) % (2 * (QUERY_HEADS // devices)) == 0


def solution(mesh):
    in_specs = (
        P("section", "expert", None),
        P("section", "expert", None),
        P("section", None, "expert", None),
        P("section", None, "expert", None),
        P("section"),
        P("section", "expert", None),
        P("section", None),
        P("section", None, None),
        P("section", "expert", None),
        P("section", "expert", None, None),
        P("section", "expert", None, None),
        P("section", "expert", None, None),
    )
    out_specs = P("section", "expert", None)
    body = shards
    if fits_one_kernel(mesh):
        body = functools.partial(fused_shards, mesh.shape["section"])
    return jax.shard_map(body, mesh=mesh, in_specs=in_specs, out_specs=out_specs, check_vma=False)
```

```python
import functools
import math

import jax
import jax.numpy as jnp
from jax import lax
from jax.experimental import pallas as pl
from jax.experimental.pallas import tpu as pltpu
from jax.sharding import PartitionSpec as P

D = 4096
QUERY_HEADS = 32
KEY_VALUE_HEADS = 2
HEAD_SIZE = 128
EXPERTS = 128
SPLIT = 4


def shifted(shard, axis, by):
    length = lax.axis_size(axis)
    return lax.ppermute(shard, axis, [(i, (i + by) % length) for i in range(length)])


def shards(
    hidden,
    queries,
    fresh_kv,
    cache_kv,
    cache_fill,
    out_proj,
    norm_gain,
    router_weight,
    expert_labels,
    gate_proj,
    up_proj,
    down_proj,
):
    devices = lax.axis_size("expert")
    device_index = lax.axis_index("expert")
    section_tokens = hidden.shape[1]
    local_cache = cache_kv.shape[2]
    stride = local_cache + section_tokens
    head_group = QUERY_HEADS // KEY_VALUE_HEADS
    scale = 1.0 / math.sqrt(HEAD_SIZE)
    fill = cache_fill[0]
    query_pos = device_index * section_tokens + jnp.arange(section_tokens, dtype=jnp.int32)
    gathered_queries = queries[0].reshape(section_tokens, KEY_VALUE_HEADS, head_group, HEAD_SIZE)
    joined_rows = jnp.concatenate([cache_kv[0], fresh_kv[0]], axis=1)

    def attend_block(carry, block_key_value, start):
        run_max, run_sum, run_acc = carry
        token_count = block_key_value.shape[1]
        row_index = start + jnp.arange(token_count, dtype=jnp.int32)
        owner = row_index // stride
        offset = row_index % stride
        cache_pos = owner * local_cache + offset
        slice_pos = owner * section_tokens + offset - local_cache
        visible = jnp.where(
            offset[None, :] < local_cache,
            cache_pos[None, :] < fill,
            slice_pos[None, :] <= query_pos[:, None],
        )
        key_matrix = block_key_value[0].reshape(token_count, KEY_VALUE_HEADS, HEAD_SIZE)
        value_matrix = block_key_value[1].reshape(token_count, KEY_VALUE_HEADS, HEAD_SIZE)
        scores = (
            jnp.einsum(
                "tgkd,rgd->tgkr", gathered_queries, key_matrix, preferred_element_type=jnp.float32
            )
            * scale
        )
        mask = visible[:, None, None, :]
        masked = jnp.where(mask, scores, -1e30)
        new_max = jnp.maximum(run_max, jnp.max(masked, axis=3))
        weights = jnp.where(mask, jnp.exp(masked - new_max[..., None]), 0.0)
        factor = jnp.exp(run_max - new_max)
        new_sum = run_sum * factor + jnp.sum(weights, axis=3)
        rounded = weights.astype(jnp.bfloat16)
        new_acc = run_acc * factor[..., None] + jnp.einsum(
            "tgkr,rgd->tgkd", rounded, value_matrix, preferred_element_type=jnp.float32
        )
        return (new_max, new_sum, new_acc)

    def attend_piece(carry, piece, start):
        token_count = piece.shape[1]
        cache_block = token_count
        while cache_block > 1024 and cache_block % 2 == 0:
            cache_block = cache_block // 2
        relay_steps = token_count // cache_block
        if relay_steps == 1:
            return attend_block(carry, piece, start)
        cache_blocks = jnp.transpose(
            piece.reshape(2, relay_steps, cache_block, KEY_VALUE_HEADS * HEAD_SIZE), (1, 0, 2, 3)
        )
        offsets = start + jnp.arange(relay_steps, dtype=jnp.int32) * cache_block

        def one_step(state, item):
            block_key_value, first = item
            return (attend_block(state, block_key_value, first), None)

        final, unused = lax.scan(one_step, carry, (cache_blocks, offsets))
        return final

    initial_maximum = jnp.full((section_tokens, KEY_VALUE_HEADS, head_group), -1e30, jnp.float32)
    initial_sum = jnp.zeros((section_tokens, KEY_VALUE_HEADS, head_group), jnp.float32)
    initial_accumulator = jnp.zeros(
        (section_tokens, KEY_VALUE_HEADS, head_group, HEAD_SIZE), jnp.float32
    )
    every_key_value = lax.all_gather(joined_rows, "expert", axis=1, tiled=True)
    final_max, final_sum, final_acc = attend_piece(
        (initial_maximum, initial_sum, initial_accumulator), every_key_value, jnp.int32(0)
    )
    attended = (
        (final_acc / final_sum[..., None])
        .reshape(section_tokens, QUERY_HEADS * HEAD_SIZE)
        .astype(jnp.bfloat16)
    )
    features = lax.all_to_all(attended, "expert", split_axis=1, concat_axis=0, tiled=True)
    partial_projected = jnp.dot(features, out_proj[0], preferred_element_type=jnp.float32)
    projected = lax.psum_scatter(
        partial_projected.astype(jnp.bfloat16), "expert", scatter_dimension=0, tiled=True
    ).astype(jnp.float32)
    mixed = hidden[0].astype(jnp.float32) + projected
    inverse = lax.rsqrt(jnp.mean(mixed * mixed, axis=1, keepdims=True) + 1e-06)
    normed = (mixed * inverse * norm_gain[0].astype(jnp.float32)[None, :]).astype(jnp.bfloat16)
    logits = jnp.dot(normed, router_weight[0], preferred_element_type=jnp.float32)
    label_rows = expert_labels[0]
    matches = label_rows[:, :, None] == jnp.arange(EXPERTS, dtype=jnp.int32)[None, None, :]
    picked = jnp.sum(jnp.where(matches, logits[:, None, :], 0.0), axis=2)
    probabilities = jax.nn.softmax(picked, axis=1)
    airborne_expert = devices // SPLIT
    hot_rows = SPLIT * max(1, section_tokens // (8 * SPLIT))
    other_rows = (section_tokens - hot_rows + airborne_expert - 2) // (airborne_expert - 1)
    capacity = SPLIT * ((max(hot_rows, other_rows) + SPLIT - 1) // SPLIT)
    airborne_mask = label_rows < airborne_expert
    selected_experts = jnp.sum(jnp.where(airborne_mask, label_rows, 0), axis=1)
    merge_results = jnp.sum(jnp.where(airborne_mask, probabilities, 0.0), axis=1)
    member = (
        selected_experts[:, None] == jnp.arange(airborne_expert, dtype=jnp.int32)[None, :]
    ).astype(jnp.int32)
    earlier = jnp.cumsum(member, axis=0) - member
    slot = jnp.sum(earlier * member, axis=1)
    code = selected_experts * capacity + slot
    table = (
        code[None, :] == jnp.arange(airborne_expert * capacity, dtype=jnp.int32)[:, None]
    ).astype(jnp.bfloat16)
    packed = (
        jnp.dot(table, normed, preferred_element_type=jnp.float32)
        .astype(jnp.bfloat16)
        .reshape(airborne_expert, capacity, D)
    )
    outgoing = jnp.repeat(packed, SPLIT, axis=0)
    received = lax.all_to_all(outgoing, "expert", split_axis=0, concat_axis=0, tiled=True)
    row_block = received.reshape(devices * capacity, D)
    gated = jnp.dot(row_block, gate_proj[0, 0], preferred_element_type=jnp.float32)
    lifted = jnp.dot(row_block, up_proj[0, 0], preferred_element_type=jnp.float32)
    activation = (jax.nn.silu(gated) * lifted).astype(jnp.bfloat16)
    partial_value = jnp.dot(
        activation, down_proj[0, 0], preferred_element_type=jnp.float32
    ).reshape(devices, capacity, D)
    returned = lax.all_to_all(
        partial_value.astype(jnp.bfloat16), "expert", split_axis=0, concat_axis=0, tiled=True
    ).astype(partial_value.dtype)
    summed = jnp.sum(returned.reshape(airborne_expert, SPLIT, capacity, D), axis=1).reshape(
        airborne_expert * capacity, D
    )
    routed = summed[code]
    result = (mixed + merge_results[:, None] * routed).astype(jnp.bfloat16)
    return shifted(result[None], "section", 1)


MESH = pl.DeviceIdType.MESH
PIECES = 4
LINE = 4


def tick_kernel(
    sizes,
    rows_ref,
    fill_ref,
    gain_ref,
    label_ref,
    query_hbm,
    hidden_hbm,
    out_proj_hbm,
    router_hbm,
    gate_hbm,
    up_hbm,
    down_hbm,
    out_ref,
    out_proj_ref,
    router_ref,
    widen_ref,
    down_ref,
    hidden_ref,
    query_all,
    rows_all,
    keys_ref,
    values_ref,
    relation_ref,
    attended_ref,
    pair_send,
    pair_recv,
    part_ref,
    inward_send,
    outward_send,
    near_recv,
    far_recv,
    normed_ref,
    mixed_ref,
    combine_ref,
    expert_send,
    expert_recv,
    routed_ref,
    back_send,
    back_recv,
    home_recv,
    result_ref,
    weight_sem,
    query_send_sem,
    query_recv_sem,
    rows_send_sem,
    rows_recv_sem,
    share_send_sem,
    share_recv_sem,
    pair_sem,
    near_sem,
    far_sem,
    fall_sem,
    norm_sem,
    expert_sem,
    back_sem,
    home_send_sem,
    home_recv_sem,
    out_sem,
):
    devices, sections, tokens, cache_rows, heads, head_group, local_experts = sizes
    chips = devices // 2
    width = hidden_ref.shape[1] // PIECES
    section = lax.axis_index("section")
    me = lax.axis_index("expert")
    chip, core = me // 2, me % 2
    partner = me + 1 - 2 * core
    next_section = (section + 1) % sections
    before_section = (section + sections - 1) % sections
    toward = jnp.where(chip < 2, 2, -2)
    inward = me + toward
    outward = (me + devices - toward) % devices
    inner = (chip == 1) | (chip == 2)
    side = chip // 2
    features = query_all.shape[2]
    units = down_ref.shape[0]

    def remote(source, target, send_sem, recv_sem, to, to_section=None):
        return pltpu.make_async_remote_copy(
            src_ref=source,
            dst_ref=target,
            send_sem=send_sem,
            recv_sem=recv_sem,
            device_id=(section if to_section is None else to_section, to),
            device_id_type=MESH,
        )

    weights = [
        pltpu.make_async_copy(source, target, weight_sem.at[at])
        for at, (source, target) in enumerate(
            [
                (out_proj_hbm.at[0], out_proj_ref),
                (hidden_hbm.at[0], hidden_ref),
                (gate_hbm.at[0, 0], widen_ref.at[:, :units]),
                (up_hbm.at[0, 0], widen_ref.at[:, units:]),
                (down_hbm.at[0, 0], down_ref),
                (router_hbm.at[0], router_ref),
            ]
        )
    ]

    def key_head(chip_at):
        return (chip_at * 2 * heads) // head_group

    def query_part(to):
        return query_hbm.at[0, :, pl.ds(pl.multiple_of(to * features, HEAD_SIZE), features)]

    own_query = pltpu.make_async_copy(query_part(me), query_all.at[me], query_recv_sem.at[0])

    for copy in weights:
        copy.start()
    own_query.start()
    rows_all[me] = rows_ref[key_head(chip)]
    barrier = pltpu.get_barrier_semaphore()
    for step in range(1, devices):
        pl.semaphore_signal(
            barrier, inc=1, device_id=(section, (me + step) % devices), device_id_type=MESH
        )
    pl.semaphore_signal(barrier, inc=1, device_id=(next_section, me), device_id_type=MESH)
    pl.semaphore_signal(barrier, inc=1, device_id=(before_section, me), device_id_type=MESH)
    pl.semaphore_wait(barrier, devices + 1)

    def query_copy(step):
        to = (me + step) % devices
        return remote(
            query_part(to),
            query_all.at[me],
            query_send_sem.at[step],
            query_recv_sem.at[step],
            to,
        )

    def rows_copy(step):
        to_chip = (chip + step) % chips
        return remote(
            rows_ref.at[key_head(to_chip)],
            rows_all.at[me],
            rows_send_sem.at[step],
            rows_recv_sem.at[step],
            2 * to_chip + core,
        )

    def share_copy(step):
        slot = 2 * ((chip + chips - step) % chips) + core
        return remote(
            rows_all.at[slot],
            rows_all.at[slot],
            share_send_sem.at[step],
            share_recv_sem.at[step],
            partner,
        )

    for step in range(1, chips):
        rows_copy(step).start()
    def send_queries():
        for step in range(1, devices):
            query_copy(step).start()

    pl.when(jnp.logical_not(inner))(send_queries)
    for step in range(chips):
        if step > 0:
            rows_copy(step).wait_recv()
        share_copy(step).start()
    for step in range(chips):
        share_copy(step).wait_recv()

    for device in range(devices):
        at = 0
        for ref in (keys_ref, values_ref):
            start = devices * cache_rows + device * tokens
            ref[start : start + tokens, :HEAD_SIZE] = rows_all[device, at : at + tokens]
            at += tokens
        for ref in (keys_ref, values_ref):
            start = device * cache_rows
            ref[start : start + cache_rows, :HEAD_SIZE] = rows_all[device, at : at + cache_rows]
            at += cache_rows
    own_query.wait()
    for copy in weights[:2]:
        copy.wait()

    fill = fill_ref[0]
    total_rows = keys_ref.shape[0]
    cached = devices * cache_rows
    group_rows = heads * tokens
    column = lax.broadcasted_iota(jnp.int32, (group_rows, total_rows), 1)
    row_token = lax.broadcasted_iota(jnp.int32, (group_rows, total_rows), 0) % tokens
    relation_ref[...] = jnp.where(column < cached, column, column - cached - row_token)
    values_ref[:, HEAD_SIZE:] = jnp.ones((total_rows, HEAD_SIZE), jnp.bfloat16)
    first_row = lax.broadcasted_iota(jnp.int32, (1, total_rows), 1)

    def home_of(step):
        return jnp.where(step % 2 == 0, step // 2, chips - 1 - step // 2)

    def piece_copy(source, target, sems, step, piece, to):
        return remote(
            source.at[step, piece],
            target.at[step, piece],
            sems.at[0, step, piece],
            sems.at[1, step, piece],
            to,
        )

    def pair_copy(step, piece):
        return piece_copy(pair_send, pair_recv, pair_sem, step, piece, partner)

    def near_copy(step, piece):
        return piece_copy(inward_send, near_recv, near_sem, step, piece, inward)

    def far_copy(step, piece):
        return piece_copy(inward_send, far_recv, far_sem, step, piece, inward)

    def fall_copy(step, piece):
        return remote(
            outward_send.at[step, piece],
            far_recv.at[step, piece],
            fall_sem.at[step, piece],
            far_sem.at[1, step, piece],
            outward,
        )

    def expert_copy(step, piece):
        return piece_copy(expert_send, expert_recv, expert_sem, step, piece, partner)

    def back_copy(step, piece):
        return piece_copy(back_send, back_recv, back_sem, step, piece, inward)

    def home_copy(step, piece, from_side):
        return remote(
            back_send.at[step, piece],
            home_recv.at[from_side, piece],
            home_send_sem.at[step, piece],
            home_recv_sem.at[from_side, piece],
            2 * home_of(step) + core,
        )

    def norm_copy(step, piece):
        return remote(
            normed_ref.at[step, piece, pl.ds(0, tokens)],
            normed_ref.at[step, piece, pl.ds(tokens, tokens)],
            norm_sem.at[0, step, piece],
            norm_sem.at[1, step, piece],
            partner,
        )

    def out_copy(piece):
        return remote(
            result_ref.at[piece],
            out_ref.at[:, pl.ds(piece * width, width)],
            out_sem.at[0, piece],
            out_sem.at[1, piece],
            me,
            next_section,
        )

    def project(step):
        home = home_of(step)
        for which in range(2):
            owner = 2 * home + (core if which == 0 else 1 - core)
            @pl.when(owner != me)
            def _():
                query_copy((me + devices - owner) % devices).wait_recv()

            scores = lax.dot_general(
                jnp.concatenate(
                    [
                        query_all[owner, :, head * HEAD_SIZE : (head + 1) * HEAD_SIZE]
                        for head in range(heads)
                    ],
                    axis=0,
                ),
                keys_ref[...],
                (((1,), (1,)), ((), ())),
                preferred_element_type=jnp.float32,
            )
            limit = jnp.where(first_row < cached, fill, owner * tokens + 1)
            masked = jnp.where(relation_ref[...] < limit, scores, -1e30)
            highest = jnp.max(masked, axis=1, keepdims=True)
            weight = jnp.exp2(
                (masked - highest) * (1.0 / (math.sqrt(HEAD_SIZE) * math.log(2.0)))
            )
            summed = jnp.dot(
                weight.astype(jnp.bfloat16), values_ref[...], preferred_element_type=jnp.float32
            )
            mean = (summed[:, :HEAD_SIZE] / summed[:, HEAD_SIZE:]).astype(jnp.bfloat16)
            for head in range(heads):
                attended_ref[
                    which * tokens : (which + 1) * tokens, head * HEAD_SIZE : (head + 1) * HEAD_SIZE
                ] = mean[head * tokens : (head + 1) * tokens]
        def ship(piece):
            @pl.when(home == chip)
            def _():
                part_ref[step, piece] += hidden_ref[
                    :, piece * width : (piece + 1) * width
                ].astype(jnp.float32)

            pair_copy(step, piece).wait_recv()
            part_ref[step, piece] += pair_recv[step, piece].astype(jnp.float32)

            @pl.when(jnp.logical_not(inner))
            def _():
                inward_send[step, piece] = part_ref[step, piece].astype(jnp.bfloat16)
                near_copy(step, piece).start()

        for piece in range(PIECES):
            product = jnp.dot(
                attended_ref[...],
                out_proj_ref[:, piece * width : (piece + 1) * width],
                preferred_element_type=jnp.float32,
            )
            part_ref[step, piece] = product[:tokens]
            pair_send[step, piece] = product[tokens:].astype(jnp.bfloat16)
            pair_copy(step, piece).start()
            if piece > 0:
                ship(piece - 1)
        ship(PIECES - 1)

    def within(step):
        return (step >= 0) & (step < chips)

    def forward(step, piece):
        near_copy(step, piece).wait_recv()
        inward_send[step, piece] = (
            part_ref[step, piece] + near_recv[step, piece].astype(jnp.float32)
        ).astype(jnp.bfloat16)
        far_copy(step, piece).start()

    def forward_first():
        for piece in range(PIECES):
            forward(0, piece)

    my_expert = (me // SPLIT).astype(jnp.float32)
    select_at = 2 * tokens + 2 * cache_rows

    def layer(step):
        home = home_of(step)

        @pl.when(step == 0)
        def _():
            for copy in weights[2:]:
                copy.wait()

        for piece in range(PIECES):
            far_copy(step, piece).wait_recv()
            part_ref[step, piece] += far_recv[step, piece].astype(jnp.float32)

            @pl.when(inner)
            def _():
                outward_send[step, piece] = part_ref[step, piece].astype(jnp.bfloat16)
                fall_copy(step, piece).start()
                part_ref[step, piece] += near_recv[step, piece].astype(jnp.float32)

        squares = jnp.zeros((tokens, 1), jnp.float32)
        for piece in range(PIECES):
            mixed = part_ref[step, piece]
            squares += jnp.sum(mixed * mixed, axis=1, keepdims=True)
        inverse = lax.rsqrt(squares / (PIECES * width) + 1e-06)
        for piece in range(PIECES):
            columns = slice(piece * width, (piece + 1) * width)
            normed_ref[step, piece, :tokens] = (
                part_ref[step, piece] * inverse * gain_ref[:, columns].astype(jnp.float32)
            ).astype(jnp.bfloat16)
            norm_copy(step, piece).start()

        @pl.when(home == chip)
        def _():
            for piece in range(PIECES):
                mixed_ref[piece] = part_ref[step, piece]
            logits = jnp.zeros((tokens, router_ref.shape[1]), jnp.float32)
            for piece in range(PIECES):
                logits += jnp.dot(
                    normed_ref[step, piece, :tokens],
                    router_ref[piece * width : (piece + 1) * width],
                    preferred_element_type=jnp.float32,
                )
            labels = label_ref[...]
            expert_at = lax.broadcasted_iota(jnp.int32, logits.shape, 1)
            picked = []
            for at in range(labels.shape[1]):
                match = labels[:, at : at + 1] == expert_at
                picked.append(jnp.sum(jnp.where(match, logits, 0.0), axis=1, keepdims=True))
            highest = picked[0]
            for value in picked[1:]:
                highest = jnp.maximum(highest, value)
            total = jnp.zeros_like(highest)
            chosen = jnp.zeros_like(highest)
            for at, value in enumerate(picked):
                weight = jnp.exp(value - highest)
                total += weight
                chosen += jnp.where(labels[:, at : at + 1] < local_experts, weight, 0.0)
            combine_ref[...] = jnp.broadcast_to(chosen / total, combine_ref.shape)

        widened = jnp.zeros((2 * tokens, 2 * units), jnp.float32)
        for piece in range(PIECES):
            norm_copy(step, piece).wait_recv()
            widened += jnp.dot(
                normed_ref[step, piece],
                widen_ref[piece * width : (piece + 1) * width],
                preferred_element_type=jnp.float32,
            )
            pl.when(inner & within(step + 1))(functools.partial(forward, step + 1, piece))
        gated, lifted = widened[:, :units], widened[:, units:]
        activation = gated / (1.0 + jnp.exp(-gated)) * lifted
        selected = jnp.concatenate(
            [
                rows_all[2 * home + core, select_at : select_at + tokens],
                rows_all[2 * home + 1 - core, select_at : select_at + tokens],
            ],
            axis=0,
        ).astype(jnp.float32)[:, :1]
        activation = jnp.where(selected == my_expert, activation, 0.0).astype(jnp.bfloat16)
        for piece in range(PIECES):
            product = jnp.dot(
                activation,
                down_ref[:, piece * width : (piece + 1) * width],
                preferred_element_type=jnp.float32,
            )
            routed_ref[step, piece] = product[:tokens]
            expert_send[step, piece] = product[tokens:].astype(jnp.bfloat16)
            expert_copy(step, piece).start()
        for piece in range(PIECES):
            expert_copy(step, piece).wait_recv()
            routed_ref[step, piece] += expert_recv[step, piece].astype(jnp.float32)

            @pl.when(jnp.logical_not(inner) & (home != chip))
            def _():
                back_send[step, piece] = routed_ref[step, piece].astype(jnp.bfloat16)
                back_copy(step, piece).start()

    def outer_chip():
        return 3 * side

    def fold(step):
        home = home_of(step)
        for piece in range(PIECES):

            @pl.when(home != outer_chip())
            def _():
                back_copy(step, piece).wait_recv()
                routed_ref[step, piece] += back_recv[step, piece].astype(jnp.float32)

            @pl.when(home != chip)
            def _():
                back_send[step, piece] = routed_ref[step, piece].astype(jnp.bfloat16)
                home_copy(step, piece, side).start()

    def finish(step):
        for piece in range(PIECES):
            for from_side in range(2):

                @pl.when(chip != from_side + 1)
                def _():
                    home_copy(step, piece, from_side).wait_recv()
                    routed_ref[step, piece] += home_recv[from_side, piece].astype(jnp.float32)

            result_ref[piece] = (
                mixed_ref[piece] + combine_ref[:, :1] * routed_ref[step, piece]
            ).astype(jnp.bfloat16)
            out_copy(piece).start()

    def turn(time, carry):
        pl.when(within(time))(lambda: project(time))
        pl.when((time == 0) & inner)(send_queries)
        pl.when((time == 0) & inner)(forward_first)
        layer_step = time - jnp.where(inner, 1, 3)
        pl.when(within(layer_step))(lambda: layer(layer_step))
        pl.when(within(time - 4) & inner)(lambda: fold(time - 4))
        ending = time - 6
        pl.when(within(ending) & (home_of(ending) == chip))(lambda: finish(ending))
        return carry

    lax.fori_loop(0, chips + 6, turn, 0)

    def drain(step, carry):
        home = home_of(step)
        for piece in range(PIECES):
            norm_copy(step, piece).wait_send()
            pair_copy(step, piece).wait_send()
            expert_copy(step, piece).wait_send()

            @pl.when(inner)
            def _():
                far_copy(step, piece).wait_send()
                fall_copy(step, piece).wait_send()

            @pl.when(jnp.logical_not(inner))
            def _():
                near_copy(step, piece).wait_send()

            @pl.when(inner & (home != chip))
            def _():
                home_copy(step, piece, side).wait_send()

            @pl.when(jnp.logical_not(inner) & (home != chip))
            def _():
                back_copy(step, piece).wait_send()

        return carry

    lax.fori_loop(0, chips, drain, 0)
    for step in range(1, chips):
        rows_copy(step).wait_send()
    for step in range(chips):
        share_copy(step).wait_send()
    for step in range(1, devices):
        query_copy(step).wait_send()
    for piece in range(PIECES):
        out_copy(piece).wait()


def fused_shards(
    sections,
    hidden,
    queries,
    fresh_kv,
    cache_kv,
    cache_fill,
    out_proj,
    norm_gain,
    router_weight,
    expert_labels,
    gate_proj,
    up_proj,
    down_proj,
):
    devices = lax.axis_size("expert")
    chips = devices // 2
    tokens, model = hidden.shape[1:]
    cache_rows = cache_kv.shape[2]
    heads = QUERY_HEADS // devices
    head_group = QUERY_HEADS // KEY_VALUE_HEADS
    local_experts = devices // SPLIT
    features = heads * HEAD_SIZE
    hidden_units = gate_proj.shape[3]
    width = model // PIECES
    labels = expert_labels[0]
    selected = jnp.sum(jnp.where(labels < local_experts, labels, 0), axis=1)

    def by_head(array, length):
        return jnp.transpose(
            array.reshape(2, length, KEY_VALUE_HEADS, HEAD_SIZE), (2, 0, 1, 3)
        ).reshape(KEY_VALUE_HEADS, 2 * length, HEAD_SIZE)

    key_rows = jnp.concatenate(
        [
            by_head(fresh_kv[0], tokens),
            by_head(cache_kv[0], cache_rows),
            jnp.broadcast_to(
                selected.astype(jnp.bfloat16)[None, :, None], (KEY_VALUE_HEADS, tokens, HEAD_SIZE)
            ),
        ],
        axis=1,
    )
    message = key_rows.shape[1]
    bf16, f32 = jnp.bfloat16, jnp.float32
    vmem = pl.BlockSpec(memory_space=pltpu.VMEM)
    anywhere = pl.BlockSpec(memory_space=pl.ANY)
    block = (chips, PIECES, tokens, width)
    dma = pltpu.SemaphoreType.DMA
    sizes = (devices, sections, tokens, cache_rows, heads, head_group, local_experts)
    total_rows = devices * (tokens + cache_rows)
    result = pl.pallas_call(
        functools.partial(tick_kernel, sizes),
        out_shape=jax.ShapeDtypeStruct((tokens, model), bf16),
        in_specs=[vmem, pl.BlockSpec(memory_space=pltpu.SMEM), vmem, vmem] + [anywhere] * 7,
        out_specs=vmem,
        scratch_shapes=[
            pltpu.VMEM((features, model), bf16),
            pltpu.VMEM(router_weight.shape[1:], bf16),
            pltpu.VMEM((model, 2 * hidden_units), bf16),
            pltpu.VMEM((hidden_units, model), bf16),
            pltpu.VMEM((tokens, model), bf16),
            pltpu.VMEM((devices, tokens, features), bf16),
            pltpu.VMEM((devices, message, HEAD_SIZE), bf16),
            pltpu.VMEM((total_rows, HEAD_SIZE), bf16),
            pltpu.VMEM((total_rows, 2 * HEAD_SIZE), bf16),
            pltpu.VMEM((heads * tokens, total_rows), jnp.int32),
            pltpu.VMEM((2 * tokens, features), bf16),
            pltpu.VMEM(block, bf16),
            pltpu.VMEM(block, bf16),
            pltpu.VMEM(block, f32),
            pltpu.VMEM(block, bf16),
            pltpu.VMEM(block, bf16),
            pltpu.VMEM(block, bf16),
            pltpu.VMEM(block, bf16),
            pltpu.VMEM((chips, PIECES, 2 * tokens, width), bf16),
            pltpu.VMEM((PIECES, tokens, width), f32),
            pltpu.VMEM((tokens, 128), f32),
            pltpu.VMEM(block, bf16),
            pltpu.VMEM(block, bf16),
            pltpu.VMEM(block, f32),
            pltpu.VMEM(block, bf16),
            pltpu.VMEM(block, bf16),
            pltpu.VMEM((2, PIECES, tokens, width), bf16),
            pltpu.VMEM((PIECES, tokens, width), bf16),
            dma((6,)),
            dma((devices,)),
            dma((devices,)),
            dma((chips,)),
            dma((chips,)),
            dma((chips,)),
            dma((chips,)),
            dma((2, chips, PIECES)),
            dma((2, chips, PIECES)),
            dma((2, chips, PIECES)),
            dma((chips, PIECES)),
            dma((2, chips, PIECES)),
            dma((2, chips, PIECES)),
            dma((2, chips, PIECES)),
            dma((chips, PIECES)),
            dma((2, PIECES)),
            dma((2, PIECES)),
        ],
        compiler_params=pltpu.CompilerParams(
            collective_id=0, has_side_effects=True, vmem_limit_bytes=60 * 2**20
        ),
    )(
        key_rows,
        cache_fill,
        norm_gain,
        labels,
        queries,
        hidden,
        out_proj,
        router_weight,
        gate_proj,
        up_proj,
        down_proj,
    )
    return result[None]


def fits_one_kernel(mesh):
    devices = mesh.shape["expert"]
    if devices != 2 * LINE or QUERY_HEADS % devices:
        return False
    return (QUERY_HEADS // KEY_VALUE_HEADS) % (2 * (QUERY_HEADS // devices)) == 0


def solution(mesh):
    in_specs = (
        P("section", "expert", None),
        P("section", "expert", None),
        P("section", None, "expert", None),
        P("section", None, "expert", None),
        P("section"),
        P("section", "expert", None),
        P("section", None),
        P("section", None, None),
        P("section", "expert", None),
        P("section", "expert", None, None),
        P("section", "expert", None, None),
        P("section", "expert", None, None),
    )
    out_specs = P("section", "expert", None)
    body = shards
    if fits_one_kernel(mesh):
        body = functools.partial(fused_shards, mesh.shape["section"])
    return jax.shard_map(body, mesh=mesh, in_specs=in_specs, out_specs=out_specs, check_vma=False)
```

```python
import functools
import math

import jax
import jax.numpy as jnp
from jax import lax
from jax.experimental import pallas as pl
from jax.experimental.pallas import tpu as pltpu
from jax.sharding import PartitionSpec as P

D = 4096
QUERY_HEADS = 32
KEY_VALUE_HEADS = 2
HEAD_SIZE = 128
EXPERTS = 128
SPLIT = 4


def shifted(shard, axis, by):
    length = lax.axis_size(axis)
    return lax.ppermute(shard, axis, [(i, (i + by) % length) for i in range(length)])


def shards(
    hidden,
    queries,
    fresh_kv,
    cache_kv,
    cache_fill,
    out_proj,
    norm_gain,
    router_weight,
    expert_labels,
    gate_proj,
    up_proj,
    down_proj,
):
    devices = lax.axis_size("expert")
    device_index = lax.axis_index("expert")
    section_tokens = hidden.shape[1]
    local_cache = cache_kv.shape[2]
    stride = local_cache + section_tokens
    head_group = QUERY_HEADS // KEY_VALUE_HEADS
    scale = 1.0 / math.sqrt(HEAD_SIZE)
    fill = cache_fill[0]
    query_pos = device_index * section_tokens + jnp.arange(section_tokens, dtype=jnp.int32)
    gathered_queries = queries[0].reshape(section_tokens, KEY_VALUE_HEADS, head_group, HEAD_SIZE)
    joined_rows = jnp.concatenate([cache_kv[0], fresh_kv[0]], axis=1)

    def attend_block(carry, block_key_value, start):
        run_max, run_sum, run_acc = carry
        token_count = block_key_value.shape[1]
        row_index = start + jnp.arange(token_count, dtype=jnp.int32)
        owner = row_index // stride
        offset = row_index % stride
        cache_pos = owner * local_cache + offset
        slice_pos = owner * section_tokens + offset - local_cache
        visible = jnp.where(
            offset[None, :] < local_cache,
            cache_pos[None, :] < fill,
            slice_pos[None, :] <= query_pos[:, None],
        )
        key_matrix = block_key_value[0].reshape(token_count, KEY_VALUE_HEADS, HEAD_SIZE)
        value_matrix = block_key_value[1].reshape(token_count, KEY_VALUE_HEADS, HEAD_SIZE)
        scores = (
            jnp.einsum(
                "tgkd,rgd->tgkr", gathered_queries, key_matrix, preferred_element_type=jnp.float32
            )
            * scale
        )
        mask = visible[:, None, None, :]
        masked = jnp.where(mask, scores, -1e30)
        new_max = jnp.maximum(run_max, jnp.max(masked, axis=3))
        weights = jnp.where(mask, jnp.exp(masked - new_max[..., None]), 0.0)
        factor = jnp.exp(run_max - new_max)
        new_sum = run_sum * factor + jnp.sum(weights, axis=3)
        rounded = weights.astype(jnp.bfloat16)
        new_acc = run_acc * factor[..., None] + jnp.einsum(
            "tgkr,rgd->tgkd", rounded, value_matrix, preferred_element_type=jnp.float32
        )
        return (new_max, new_sum, new_acc)

    def attend_piece(carry, piece, start):
        token_count = piece.shape[1]
        cache_block = token_count
        while cache_block > 1024 and cache_block % 2 == 0:
            cache_block = cache_block // 2
        relay_steps = token_count // cache_block
        if relay_steps == 1:
            return attend_block(carry, piece, start)
        cache_blocks = jnp.transpose(
            piece.reshape(2, relay_steps, cache_block, KEY_VALUE_HEADS * HEAD_SIZE), (1, 0, 2, 3)
        )
        offsets = start + jnp.arange(relay_steps, dtype=jnp.int32) * cache_block

        def one_step(state, item):
            block_key_value, first = item
            return (attend_block(state, block_key_value, first), None)

        final, unused = lax.scan(one_step, carry, (cache_blocks, offsets))
        return final

    initial_maximum = jnp.full((section_tokens, KEY_VALUE_HEADS, head_group), -1e30, jnp.float32)
    initial_sum = jnp.zeros((section_tokens, KEY_VALUE_HEADS, head_group), jnp.float32)
    initial_accumulator = jnp.zeros(
        (section_tokens, KEY_VALUE_HEADS, head_group, HEAD_SIZE), jnp.float32
    )
    every_key_value = lax.all_gather(joined_rows, "expert", axis=1, tiled=True)
    final_max, final_sum, final_acc = attend_piece(
        (initial_maximum, initial_sum, initial_accumulator), every_key_value, jnp.int32(0)
    )
    attended = (
        (final_acc / final_sum[..., None])
        .reshape(section_tokens, QUERY_HEADS * HEAD_SIZE)
        .astype(jnp.bfloat16)
    )
    features = lax.all_to_all(attended, "expert", split_axis=1, concat_axis=0, tiled=True)
    partial_projected = jnp.dot(features, out_proj[0], preferred_element_type=jnp.float32)
    projected = lax.psum_scatter(
        partial_projected.astype(jnp.bfloat16), "expert", scatter_dimension=0, tiled=True
    ).astype(jnp.float32)
    mixed = hidden[0].astype(jnp.float32) + projected
    inverse = lax.rsqrt(jnp.mean(mixed * mixed, axis=1, keepdims=True) + 1e-06)
    normed = (mixed * inverse * norm_gain[0].astype(jnp.float32)[None, :]).astype(jnp.bfloat16)
    logits = jnp.dot(normed, router_weight[0], preferred_element_type=jnp.float32)
    label_rows = expert_labels[0]
    matches = label_rows[:, :, None] == jnp.arange(EXPERTS, dtype=jnp.int32)[None, None, :]
    picked = jnp.sum(jnp.where(matches, logits[:, None, :], 0.0), axis=2)
    probabilities = jax.nn.softmax(picked, axis=1)
    airborne_expert = devices // SPLIT
    hot_rows = SPLIT * max(1, section_tokens // (8 * SPLIT))
    other_rows = (section_tokens - hot_rows + airborne_expert - 2) // (airborne_expert - 1)
    capacity = SPLIT * ((max(hot_rows, other_rows) + SPLIT - 1) // SPLIT)
    airborne_mask = label_rows < airborne_expert
    selected_experts = jnp.sum(jnp.where(airborne_mask, label_rows, 0), axis=1)
    merge_results = jnp.sum(jnp.where(airborne_mask, probabilities, 0.0), axis=1)
    member = (
        selected_experts[:, None] == jnp.arange(airborne_expert, dtype=jnp.int32)[None, :]
    ).astype(jnp.int32)
    earlier = jnp.cumsum(member, axis=0) - member
    slot = jnp.sum(earlier * member, axis=1)
    code = selected_experts * capacity + slot
    table = (
        code[None, :] == jnp.arange(airborne_expert * capacity, dtype=jnp.int32)[:, None]
    ).astype(jnp.bfloat16)
    packed = (
        jnp.dot(table, normed, preferred_element_type=jnp.float32)
        .astype(jnp.bfloat16)
        .reshape(airborne_expert, capacity, D)
    )
    outgoing = jnp.repeat(packed, SPLIT, axis=0)
    received = lax.all_to_all(outgoing, "expert", split_axis=0, concat_axis=0, tiled=True)
    row_block = received.reshape(devices * capacity, D)
    gated = jnp.dot(row_block, gate_proj[0, 0], preferred_element_type=jnp.float32)
    lifted = jnp.dot(row_block, up_proj[0, 0], preferred_element_type=jnp.float32)
    activation = (jax.nn.silu(gated) * lifted).astype(jnp.bfloat16)
    partial_value = jnp.dot(
        activation, down_proj[0, 0], preferred_element_type=jnp.float32
    ).reshape(devices, capacity, D)
    returned = lax.all_to_all(
        partial_value.astype(jnp.bfloat16), "expert", split_axis=0, concat_axis=0, tiled=True
    ).astype(partial_value.dtype)
    summed = jnp.sum(returned.reshape(airborne_expert, SPLIT, capacity, D), axis=1).reshape(
        airborne_expert * capacity, D
    )
    routed = summed[code]
    result = (mixed + merge_results[:, None] * routed).astype(jnp.bfloat16)
    return shifted(result[None], "section", 1)


MESH = pl.DeviceIdType.MESH
PIECES = 8
LINE = 4


def tick_kernel(
    sizes,
    rows_ref,
    fill_ref,
    gain_ref,
    label_ref,
    query_hbm,
    hidden_hbm,
    out_proj_hbm,
    router_hbm,
    gate_hbm,
    up_hbm,
    down_hbm,
    out_ref,
    out_proj_ref,
    router_ref,
    widen_ref,
    down_ref,
    hidden_ref,
    query_all,
    rows_all,
    keys_ref,
    values_ref,
    relation_ref,
    attended_ref,
    pair_send,
    pair_recv,
    part_ref,
    inward_send,
    outward_send,
    near_recv,
    far_recv,
    normed_ref,
    mixed_ref,
    combine_ref,
    expert_send,
    expert_recv,
    routed_ref,
    back_send,
    back_recv,
    home_recv,
    result_ref,
    weight_sem,
    query_send_sem,
    query_recv_sem,
    rows_send_sem,
    rows_recv_sem,
    share_send_sem,
    share_recv_sem,
    pair_sem,
    near_sem,
    far_sem,
    fall_sem,
    norm_sem,
    expert_sem,
    back_sem,
    home_send_sem,
    home_recv_sem,
    out_sem,
):
    devices, sections, tokens, cache_rows, heads, head_group, local_experts = sizes
    chips = devices // 2
    width = hidden_ref.shape[1] // PIECES
    section = lax.axis_index("section")
    me = lax.axis_index("expert")
    chip, core = me // 2, me % 2
    partner = me + 1 - 2 * core
    next_section = (section + 1) % sections
    before_section = (section + sections - 1) % sections
    toward = jnp.where(chip < 2, 2, -2)
    inward = me + toward
    outward = (me + devices - toward) % devices
    inner = (chip == 1) | (chip == 2)
    side = chip // 2
    features = query_all.shape[2]
    units = down_ref.shape[0]

    def remote(source, target, send_sem, recv_sem, to, to_section=None):
        return pltpu.make_async_remote_copy(
            src_ref=source,
            dst_ref=target,
            send_sem=send_sem,
            recv_sem=recv_sem,
            device_id=(section if to_section is None else to_section, to),
            device_id_type=MESH,
        )

    weights = [
        pltpu.make_async_copy(source, target, weight_sem.at[at])
        for at, (source, target) in enumerate(
            [
                (out_proj_hbm.at[0], out_proj_ref),
                (hidden_hbm.at[0], hidden_ref),
                (gate_hbm.at[0, 0], widen_ref.at[:, :units]),
                (up_hbm.at[0, 0], widen_ref.at[:, units:]),
                (down_hbm.at[0, 0], down_ref),
                (router_hbm.at[0], router_ref),
            ]
        )
    ]

    def key_head(chip_at):
        return (chip_at * 2 * heads) // head_group

    def query_part(to):
        return query_hbm.at[0, :, pl.ds(pl.multiple_of(to * features, HEAD_SIZE), features)]

    own_query = pltpu.make_async_copy(query_part(me), query_all.at[me], query_recv_sem.at[0])

    for copy in weights:
        copy.start()
    own_query.start()
    rows_all[me] = rows_ref[key_head(chip)]
    barrier = pltpu.get_barrier_semaphore()
    for step in range(1, devices):
        pl.semaphore_signal(
            barrier, inc=1, device_id=(section, (me + step) % devices), device_id_type=MESH
        )
    pl.semaphore_signal(barrier, inc=1, device_id=(next_section, me), device_id_type=MESH)
    pl.semaphore_signal(barrier, inc=1, device_id=(before_section, me), device_id_type=MESH)
    pl.semaphore_wait(barrier, devices + 1)

    def query_copy(step):
        to = (me + step) % devices
        return remote(
            query_part(to),
            query_all.at[me],
            query_send_sem.at[step],
            query_recv_sem.at[step],
            to,
        )

    def rows_copy(step):
        to_chip = (chip + step) % chips
        return remote(
            rows_ref.at[key_head(to_chip)],
            rows_all.at[me],
            rows_send_sem.at[step],
            rows_recv_sem.at[step],
            2 * to_chip + core,
        )

    def share_copy(step):
        slot = 2 * ((chip + chips - step) % chips) + core
        return remote(
            rows_all.at[slot],
            rows_all.at[slot],
            share_send_sem.at[step],
            share_recv_sem.at[step],
            partner,
        )

    for step in range(1, chips):
        rows_copy(step).start()
    def send_queries():
        for step in range(1, devices):
            query_copy(step).start()

    pl.when(jnp.logical_not(inner))(send_queries)
    for step in range(chips):
        if step > 0:
            rows_copy(step).wait_recv()
        share_copy(step).start()
    for step in range(chips):
        share_copy(step).wait_recv()

    for device in range(devices):
        at = 0
        for ref in (keys_ref, values_ref):
            start = devices * cache_rows + device * tokens
            ref[start : start + tokens, :HEAD_SIZE] = rows_all[device, at : at + tokens]
            at += tokens
        for ref in (keys_ref, values_ref):
            start = device * cache_rows
            ref[start : start + cache_rows, :HEAD_SIZE] = rows_all[device, at : at + cache_rows]
            at += cache_rows
    own_query.wait()
    for copy in weights[:2]:
        copy.wait()

    fill = fill_ref[0]
    total_rows = keys_ref.shape[0]
    cached = devices * cache_rows
    group_rows = heads * tokens
    column = lax.broadcasted_iota(jnp.int32, (group_rows, total_rows), 1)
    row_token = lax.broadcasted_iota(jnp.int32, (group_rows, total_rows), 0) % tokens
    relation_ref[...] = jnp.where(column < cached, column, column - cached - row_token)
    values_ref[:, HEAD_SIZE:] = jnp.ones((total_rows, HEAD_SIZE), jnp.bfloat16)
    first_row = lax.broadcasted_iota(jnp.int32, (1, total_rows), 1)

    def home_of(step):
        return jnp.where(step % 2 == 0, step // 2, chips - 1 - step // 2)

    def piece_copy(source, target, sems, step, piece, to):
        return remote(
            source.at[step, piece],
            target.at[step, piece],
            sems.at[0, step, piece],
            sems.at[1, step, piece],
            to,
        )

    def pair_copy(step, piece):
        return piece_copy(pair_send, pair_recv, pair_sem, step, piece, partner)

    def near_copy(step, piece):
        return piece_copy(inward_send, near_recv, near_sem, step, piece, inward)

    def far_copy(step, piece):
        return piece_copy(inward_send, far_recv, far_sem, step, piece, inward)

    def fall_copy(step, piece):
        return remote(
            outward_send.at[step, piece],
            far_recv.at[step, piece],
            fall_sem.at[step, piece],
            far_sem.at[1, step, piece],
            outward,
        )

    def expert_copy(step, piece):
        return piece_copy(expert_send, expert_recv, expert_sem, step, piece, partner)

    def back_copy(step, piece):
        return piece_copy(back_send, back_recv, back_sem, step, piece, inward)

    def home_copy(step, piece, from_side):
        return remote(
            back_send.at[step, piece],
            home_recv.at[from_side, piece],
            home_send_sem.at[step, piece],
            home_recv_sem.at[from_side, piece],
            2 * home_of(step) + core,
        )

    def norm_copy(step, piece):
        return remote(
            normed_ref.at[step, piece, pl.ds(0, tokens)],
            normed_ref.at[step, piece, pl.ds(tokens, tokens)],
            norm_sem.at[0, step, piece],
            norm_sem.at[1, step, piece],
            partner,
        )

    def out_copy(piece):
        return remote(
            result_ref.at[piece],
            out_ref.at[:, pl.ds(piece * width, width)],
            out_sem.at[0, piece],
            out_sem.at[1, piece],
            me,
            next_section,
        )

    def project(step):
        home = home_of(step)
        for which in range(2):
            owner = 2 * home + (core if which == 0 else 1 - core)
            @pl.when(owner != me)
            def _():
                query_copy((me + devices - owner) % devices).wait_recv()

            scores = lax.dot_general(
                jnp.concatenate(
                    [
                        query_all[owner, :, head * HEAD_SIZE : (head + 1) * HEAD_SIZE]
                        for head in range(heads)
                    ],
                    axis=0,
                ),
                keys_ref[...],
                (((1,), (1,)), ((), ())),
                preferred_element_type=jnp.float32,
            )
            limit = jnp.where(first_row < cached, fill, owner * tokens + 1)
            masked = jnp.where(relation_ref[...] < limit, scores, -1e30)
            highest = jnp.max(masked, axis=1, keepdims=True)
            weight = jnp.exp2(
                (masked - highest) * (1.0 / (math.sqrt(HEAD_SIZE) * math.log(2.0)))
            )
            summed = jnp.dot(
                weight.astype(jnp.bfloat16), values_ref[...], preferred_element_type=jnp.float32
            )
            mean = (summed[:, :HEAD_SIZE] / summed[:, HEAD_SIZE:]).astype(jnp.bfloat16)
            for head in range(heads):
                attended_ref[
                    which * tokens : (which + 1) * tokens, head * HEAD_SIZE : (head + 1) * HEAD_SIZE
                ] = mean[head * tokens : (head + 1) * tokens]
        def ship(piece):
            @pl.when(home == chip)
            def _():
                part_ref[step, piece] += hidden_ref[
                    :, piece * width : (piece + 1) * width
                ].astype(jnp.float32)

            pair_copy(step, piece).wait_recv()
            part_ref[step, piece] += pair_recv[step, piece].astype(jnp.float32)

            @pl.when(jnp.logical_not(inner))
            def _():
                inward_send[step, piece] = part_ref[step, piece].astype(jnp.bfloat16)
                near_copy(step, piece).start()

        for piece in range(PIECES):
            product = jnp.dot(
                attended_ref[...],
                out_proj_ref[:, piece * width : (piece + 1) * width],
                preferred_element_type=jnp.float32,
            )
            part_ref[step, piece] = product[:tokens]
            pair_send[step, piece] = product[tokens:].astype(jnp.bfloat16)
            pair_copy(step, piece).start()
            if piece > 0:
                ship(piece - 1)
        ship(PIECES - 1)

    def within(step):
        return (step >= 0) & (step < chips)

    def forward(step, piece):
        near_copy(step, piece).wait_recv()
        inward_send[step, piece] = (
            part_ref[step, piece] + near_recv[step, piece].astype(jnp.float32)
        ).astype(jnp.bfloat16)
        far_copy(step, piece).start()

    def forward_first():
        for piece in range(PIECES):
            forward(0, piece)

    my_expert = (me // SPLIT).astype(jnp.float32)
    select_at = 2 * tokens + 2 * cache_rows

    def layer(step):
        home = home_of(step)

        @pl.when(step == 0)
        def _():
            for copy in weights[2:]:
                copy.wait()

        for piece in range(PIECES):
            far_copy(step, piece).wait_recv()
            part_ref[step, piece] += far_recv[step, piece].astype(jnp.float32)

            @pl.when(inner)
            def _():
                outward_send[step, piece] = part_ref[step, piece].astype(jnp.bfloat16)
                fall_copy(step, piece).start()
                part_ref[step, piece] += near_recv[step, piece].astype(jnp.float32)

        squares = jnp.zeros((tokens, 1), jnp.float32)
        for piece in range(PIECES):
            mixed = part_ref[step, piece]
            squares += jnp.sum(mixed * mixed, axis=1, keepdims=True)
        inverse = lax.rsqrt(squares / (PIECES * width) + 1e-06)
        for piece in range(PIECES):
            columns = slice(piece * width, (piece + 1) * width)
            normed_ref[step, piece, :tokens] = (
                part_ref[step, piece] * inverse * gain_ref[:, columns].astype(jnp.float32)
            ).astype(jnp.bfloat16)
            norm_copy(step, piece).start()

        @pl.when(home == chip)
        def _():
            for piece in range(PIECES):
                mixed_ref[piece] = part_ref[step, piece]
            logits = jnp.zeros((tokens, router_ref.shape[1]), jnp.float32)
            for piece in range(PIECES):
                logits += jnp.dot(
                    normed_ref[step, piece, :tokens],
                    router_ref[piece * width : (piece + 1) * width],
                    preferred_element_type=jnp.float32,
                )
            labels = label_ref[...]
            expert_at = lax.broadcasted_iota(jnp.int32, logits.shape, 1)
            picked = []
            for at in range(labels.shape[1]):
                match = labels[:, at : at + 1] == expert_at
                picked.append(jnp.sum(jnp.where(match, logits, 0.0), axis=1, keepdims=True))
            highest = picked[0]
            for value in picked[1:]:
                highest = jnp.maximum(highest, value)
            total = jnp.zeros_like(highest)
            chosen = jnp.zeros_like(highest)
            for at, value in enumerate(picked):
                weight = jnp.exp(value - highest)
                total += weight
                chosen += jnp.where(labels[:, at : at + 1] < local_experts, weight, 0.0)
            combine_ref[...] = jnp.broadcast_to(chosen / total, combine_ref.shape)

        widened = jnp.zeros((2 * tokens, 2 * units), jnp.float32)
        for piece in range(PIECES):
            norm_copy(step, piece).wait_recv()
            widened += jnp.dot(
                normed_ref[step, piece],
                widen_ref[piece * width : (piece + 1) * width],
                preferred_element_type=jnp.float32,
            )
            pl.when(inner & within(step + 1))(functools.partial(forward, step + 1, piece))
        gated, lifted = widened[:, :units], widened[:, units:]
        activation = gated / (1.0 + jnp.exp(-gated)) * lifted
        selected = jnp.concatenate(
            [
                rows_all[2 * home + core, select_at : select_at + tokens],
                rows_all[2 * home + 1 - core, select_at : select_at + tokens],
            ],
            axis=0,
        ).astype(jnp.float32)[:, :1]
        activation = jnp.where(selected == my_expert, activation, 0.0).astype(jnp.bfloat16)
        for piece in range(PIECES):
            product = jnp.dot(
                activation,
                down_ref[:, piece * width : (piece + 1) * width],
                preferred_element_type=jnp.float32,
            )
            routed_ref[step, piece] = product[:tokens]
            expert_send[step, piece] = product[tokens:].astype(jnp.bfloat16)
            expert_copy(step, piece).start()
        for piece in range(PIECES):
            expert_copy(step, piece).wait_recv()
            routed_ref[step, piece] += expert_recv[step, piece].astype(jnp.float32)

            @pl.when(jnp.logical_not(inner) & (home != chip))
            def _():
                back_send[step, piece] = routed_ref[step, piece].astype(jnp.bfloat16)
                back_copy(step, piece).start()

    def outer_chip():
        return 3 * side

    def fold(step):
        home = home_of(step)
        for piece in range(PIECES):

            @pl.when(home != outer_chip())
            def _():
                back_copy(step, piece).wait_recv()
                routed_ref[step, piece] += back_recv[step, piece].astype(jnp.float32)

            @pl.when(home != chip)
            def _():
                back_send[step, piece] = routed_ref[step, piece].astype(jnp.bfloat16)
                home_copy(step, piece, side).start()

    def finish(step):
        for piece in range(PIECES):
            for from_side in range(2):

                @pl.when(chip != from_side + 1)
                def _():
                    home_copy(step, piece, from_side).wait_recv()
                    routed_ref[step, piece] += home_recv[from_side, piece].astype(jnp.float32)

            result_ref[piece] = (
                mixed_ref[piece] + combine_ref[:, :1] * routed_ref[step, piece]
            ).astype(jnp.bfloat16)
            out_copy(piece).start()

    def turn(time, carry):
        pl.when(within(time))(lambda: project(time))
        pl.when((time == 0) & inner)(send_queries)
        pl.when((time == 0) & inner)(forward_first)
        layer_step = time - jnp.where(inner, 1, 3)
        pl.when(within(layer_step))(lambda: layer(layer_step))
        pl.when(within(time - 4) & inner)(lambda: fold(time - 4))
        ending = time - 6
        pl.when(within(ending) & (home_of(ending) == chip))(lambda: finish(ending))
        return carry

    lax.fori_loop(0, chips + 6, turn, 0)

    def drain(step, carry):
        home = home_of(step)
        for piece in range(PIECES):
            norm_copy(step, piece).wait_send()
            pair_copy(step, piece).wait_send()
            expert_copy(step, piece).wait_send()

            @pl.when(inner)
            def _():
                far_copy(step, piece).wait_send()
                fall_copy(step, piece).wait_send()

            @pl.when(jnp.logical_not(inner))
            def _():
                near_copy(step, piece).wait_send()

            @pl.when(inner & (home != chip))
            def _():
                home_copy(step, piece, side).wait_send()

            @pl.when(jnp.logical_not(inner) & (home != chip))
            def _():
                back_copy(step, piece).wait_send()

        return carry

    lax.fori_loop(0, chips, drain, 0)
    for step in range(1, chips):
        rows_copy(step).wait_send()
    for step in range(chips):
        share_copy(step).wait_send()
    for step in range(1, devices):
        query_copy(step).wait_send()
    for piece in range(PIECES):
        out_copy(piece).wait()


def fused_shards(
    sections,
    hidden,
    queries,
    fresh_kv,
    cache_kv,
    cache_fill,
    out_proj,
    norm_gain,
    router_weight,
    expert_labels,
    gate_proj,
    up_proj,
    down_proj,
):
    devices = lax.axis_size("expert")
    chips = devices // 2
    tokens, model = hidden.shape[1:]
    cache_rows = cache_kv.shape[2]
    heads = QUERY_HEADS // devices
    head_group = QUERY_HEADS // KEY_VALUE_HEADS
    local_experts = devices // SPLIT
    features = heads * HEAD_SIZE
    hidden_units = gate_proj.shape[3]
    width = model // PIECES
    labels = expert_labels[0]
    selected = jnp.sum(jnp.where(labels < local_experts, labels, 0), axis=1)

    def by_head(array, length):
        return jnp.transpose(
            array.reshape(2, length, KEY_VALUE_HEADS, HEAD_SIZE), (2, 0, 1, 3)
        ).reshape(KEY_VALUE_HEADS, 2 * length, HEAD_SIZE)

    key_rows = jnp.concatenate(
        [
            by_head(fresh_kv[0], tokens),
            by_head(cache_kv[0], cache_rows),
            jnp.broadcast_to(
                selected.astype(jnp.bfloat16)[None, :, None], (KEY_VALUE_HEADS, tokens, HEAD_SIZE)
            ),
        ],
        axis=1,
    )
    message = key_rows.shape[1]
    bf16, f32 = jnp.bfloat16, jnp.float32
    vmem = pl.BlockSpec(memory_space=pltpu.VMEM)
    anywhere = pl.BlockSpec(memory_space=pl.ANY)
    block = (chips, PIECES, tokens, width)
    dma = pltpu.SemaphoreType.DMA
    sizes = (devices, sections, tokens, cache_rows, heads, head_group, local_experts)
    total_rows = devices * (tokens + cache_rows)
    result = pl.pallas_call(
        functools.partial(tick_kernel, sizes),
        out_shape=jax.ShapeDtypeStruct((tokens, model), bf16),
        in_specs=[vmem, pl.BlockSpec(memory_space=pltpu.SMEM), vmem, vmem] + [anywhere] * 7,
        out_specs=vmem,
        scratch_shapes=[
            pltpu.VMEM((features, model), bf16),
            pltpu.VMEM(router_weight.shape[1:], bf16),
            pltpu.VMEM((model, 2 * hidden_units), bf16),
            pltpu.VMEM((hidden_units, model), bf16),
            pltpu.VMEM((tokens, model), bf16),
            pltpu.VMEM((devices, tokens, features), bf16),
            pltpu.VMEM((devices, message, HEAD_SIZE), bf16),
            pltpu.VMEM((total_rows, HEAD_SIZE), bf16),
            pltpu.VMEM((total_rows, 2 * HEAD_SIZE), bf16),
            pltpu.VMEM((heads * tokens, total_rows), jnp.int32),
            pltpu.VMEM((2 * tokens, features), bf16),
            pltpu.VMEM(block, bf16),
            pltpu.VMEM(block, bf16),
            pltpu.VMEM(block, f32),
            pltpu.VMEM(block, bf16),
            pltpu.VMEM(block, bf16),
            pltpu.VMEM(block, bf16),
            pltpu.VMEM(block, bf16),
            pltpu.VMEM((chips, PIECES, 2 * tokens, width), bf16),
            pltpu.VMEM((PIECES, tokens, width), f32),
            pltpu.VMEM((tokens, 128), f32),
            pltpu.VMEM(block, bf16),
            pltpu.VMEM(block, bf16),
            pltpu.VMEM(block, f32),
            pltpu.VMEM(block, bf16),
            pltpu.VMEM(block, bf16),
            pltpu.VMEM((2, PIECES, tokens, width), bf16),
            pltpu.VMEM((PIECES, tokens, width), bf16),
            dma((6,)),
            dma((devices,)),
            dma((devices,)),
            dma((chips,)),
            dma((chips,)),
            dma((chips,)),
            dma((chips,)),
            dma((2, chips, PIECES)),
            dma((2, chips, PIECES)),
            dma((2, chips, PIECES)),
            dma((chips, PIECES)),
            dma((2, chips, PIECES)),
            dma((2, chips, PIECES)),
            dma((2, chips, PIECES)),
            dma((chips, PIECES)),
            dma((2, PIECES)),
            dma((2, PIECES)),
        ],
        compiler_params=pltpu.CompilerParams(
            collective_id=0, has_side_effects=True, vmem_limit_bytes=60 * 2**20
        ),
    )(
        key_rows,
        cache_fill,
        norm_gain,
        labels,
        queries,
        hidden,
        out_proj,
        router_weight,
        gate_proj,
        up_proj,
        down_proj,
    )
    return result[None]


def fits_one_kernel(mesh):
    devices = mesh.shape["expert"]
    if devices != 2 * LINE or QUERY_HEADS % devices:
        return False
    return (QUERY_HEADS // KEY_VALUE_HEADS) % (2 * (QUERY_HEADS // devices)) == 0


def solution(mesh):
    in_specs = (
        P("section", "expert", None),
        P("section", "expert", None),
        P("section", None, "expert", None),
        P("section", None, "expert", None),
        P("section"),
        P("section", "expert", None),
        P("section", None),
        P("section", None, None),
        P("section", "expert", None),
        P("section", "expert", None, None),
        P("section", "expert", None, None),
        P("section", "expert", None, None),
    )
    out_specs = P("section", "expert", None)
    body = shards
    if fits_one_kernel(mesh):
        body = functools.partial(fused_shards, mesh.shape["section"])
    return jax.shard_map(body, mesh=mesh, in_specs=in_specs, out_specs=out_specs, check_vma=False)
```
